256 devices in a mesh: outer: 8 (over z_hi, y), inner: 32 (over z_lo, x, core).
Axes of the slice: x: 4, y: 4, z: 8 (z_hi: 2, z_lo: 4; z = z_hi * 4 + z_lo), core: 2. Of those that a mesh axis runs over, the one named last changes fastest.
Arguments:
- inputs: bfloat16 [4096, 6144], P('outer'), may hold values from -6 to 6
- act_grad: bfloat16 [4096, 24576], P('outer', 'inner'), may hold values from -6 to 6
- in_codes: bfloat16 [6144, 24576], P('outer', 'inner'), may hold values from -6 to 6
- in_scales: bfloat16 [6144], P('outer'), may hold values from 0.0038146973 to 0.038085938
Outputs:
- input_grad: bfloat16 [4096, 6144], P(('outer', 'inner'))
- in_grad: float32 [6144, 24576], P('outer', 'inner')
The draws below stay inside these ranges and needn't reach their ends.
All inputs are finite; a program needn't handle non-finite values.
Results may differ from the reference program's by a relative error of at most 0.0065.
Values may be sent and summed in bfloat16 or wider, within the bound.
A program may use at most 128 MiB of HBM per device.

```python
import math
import jax
import jax.numpy as jnp
from jax import lax

D = 6144
FF = 24576
TOK_DEV = 512
TOKENS = 4096
N_OUTER = 8


def spiked(array, rng, source, target, shards_of, factor):
    def block_of(dim):
        return (jnp.arange(array.shape[dim]) // (array.shape[dim] // shards_of)).reshape((-1,) + (1,) * (array.ndim - 1 - dim))

    first = jax.random.permutation(rng, shards_of)[block_of(target)]
    far = (block_of(target) + shards_of // 2) % shards_of
    return jnp.where((block_of(source) == first) | (block_of(source) == far), factor * array, array)


def levels(rng, dims, shards, smallest, top_value):
    level = 1.0
    for axis_at, shards_of in shards:
        heights = jax.random.uniform(jax.random.fold_in(jax.random.fold_in(rng, 6), axis_at), (shards_of,), jnp.float32, smallest / len(shards), top_value / len(shards))
        level = level * jnp.repeat(jnp.exp(heights), dims[axis_at] // shards_of).reshape((-1,) + (1,) * (len(dims) - 1 - axis_at))
    return level


def noise(stream_key, shape, spread, most, cuts=(), kind=jnp.bfloat16):
    gain = levels(stream_key, shape, cuts, -0.22, 0.18) if cuts else 1.0
    array = jax.random.normal(stream_key, shape, jnp.float32) * spread * gain
    return jnp.minimum(jnp.maximum(array, -most), most).astype(kind)


def bell_draw_with(stream_key, dims, deviation, most, cuts, heavy, held_as=jnp.bfloat16):
    array = deviation * jax.random.normal(stream_key, dims, jnp.float32)
    if cuts:
        array = array * levels(stream_key, dims, cuts, -0.22, 0.18)
    return jnp.clip(spiked(array, jax.random.fold_in(stream_key, 3), *heavy), -most, most).astype(held_as)


def setup_inputs(seed: int = 0) -> dict:
    arg_keys = jax.random.split(jax.random.key(seed), 5)
    return {
        "inputs": bell_draw_with(arg_keys[0], (TOKENS, D), 1.0, 6.0, ((0, 8),), (0, 1, 8, 2.0)),
        "act_grad": bell_draw_with(arg_keys[1], (TOKENS, FF), 1.0, 6.0, ((0, 8), (1, 32)), (1, 0, 32, 2.75)),
        "in_codes": noise(arg_keys[2], (D, FF), 1.0, 6.0, ((0, 8), (1, 32))),
        "in_scales": jnp.clip(jnp.exp(math.log(0.038085938) - 2.300984 * jax.random.uniform(arg_keys[3], (D,), jnp.float32) ** levels(arg_keys[3], (D,), ((0, 8),), -0.2, 0.2)), 0.0038146973, 0.038085938).astype(jnp.bfloat16),
    }


coef = 0.7978845608
cubic = 0.044715


def gelu_slope(value):
    tangent = jnp.tanh(coef * (value + cubic * value * value * value))
    return 0.5 * (1.0 + tangent) + 0.5 * value * (1.0 - tangent * tangent) * coef * (1.0 + 3.0 * cubic * value * value)


def reference(inputs, act_grad, in_codes, in_scales):
    w_in = (in_codes.astype(jnp.float32) * in_scales.astype(jnp.float32)[:, None]).astype(jnp.bfloat16)
    hidden = jnp.dot(inputs, w_in, preferred_element_type=jnp.float32)
    hid_grad = (act_grad.astype(jnp.float32) * gelu_slope(hidden)).astype(jnp.bfloat16)
    input_grad = lax.dot_general(hid_grad, w_in, (((1,), (1,)), ((), ())), preferred_element_type=jnp.float32).astype(jnp.bfloat16)
    shaped = (inputs.reshape(N_OUTER, TOK_DEV, D), hid_grad.reshape(N_OUTER, TOK_DEV, FF))
    zeros = jnp.zeros((D, FF), jnp.float32)

    def outer_step(total, pieces):
        rows_in, rows_hid = pieces
        term = lax.dot_general(rows_in, rows_hid, (((0,), (0,)), ((), ())), preferred_element_type=jnp.float32)
        return total + term, None

    total = lax.scan(outer_step, zeros, shaped)[0] / N_OUTER
    return input_grad, total
```

```python
import functools

import jax
import jax.numpy as jnp
from jax import lax
from jax.experimental import pallas as pl
from jax.experimental.pallas import tpu as pltpu
from jax.sharding import PartitionSpec as P

coef = 0.7978845608
cubic = 0.044715

MESH = pl.DeviceIdType.MESH
F32 = jnp.float32
BF16 = jnp.bfloat16

F = 3
T = 4
K = F * T
FC = 256
TC = 128
DB = 768
DP = 1536
COLS = 256

O_X1, O_X2, O_S3, O_S4, O_S5, O_S6, O_S7, O_S8, O_R1, O_R2, O_R3 = 0, 1, 2, 3, 5, 7, 8, 10, 9, 10, 11
STEPS = K + O_R3


def gelu_slope(value):
    tangent = jnp.tanh(coef * (value + cubic * value * value * value))
    return 0.5 * (1.0 + tangent) + 0.5 * value * (1.0 - tangent * tangent) * coef * (
        1.0 + 3.0 * cubic * value * value
    )


def kernel(
    x_hbm, act_hbm, w_hbm, ig_ref, gw_hbm,
    xs, ws, act, send_b, recv_b, keep, send_z, recv_z, hg, term,
    acc, send_c, recv_c, send_x, recv_x, keep_x, send_l, recv_l, keep_l,
    send_f, fin, send_a, recv_a, gout,
    sem_own, sem_wo, sem_act, sem_gw,
    xb_s, xb_r, xz_s, xz_r, xd_s, xd_r, xx_s, xx_r, xc_s, xc_r, xe_s, xe_r,
    w_s, w_r, b_s, b_r, z_s, z_r, gz_s, gz_r, g0_s, g0_r, g1_s, g1_r,
    a_s, a_r, c_s, c_r, rx_s, rx_r, l_s, l_r, f_s, f_r,
):
    o = lax.axis_index("outer")
    i = lax.axis_index("inner")
    h, y = o // 4, o % 4
    l, x, c = i // 8, (i // 2) % 4, i % 2
    pair, side = y // 2, y % 2
    h2, yb = 1 - h, 3 - y
    ya = pair * 2 + (1 - side)

    def at(hh, yy, ll, xx, cc):
        return (hh * 4 + yy, (ll * 4 + xx) * 2 + cc)

    dev_a = at(h, ya, l, x, c)
    dev_b = at(h, yb, l, x, c)
    dev_z = at(h2, y, l, x, c)
    dev_d = at(h2, yb, l, x, c)
    dev_c = at(h, y, l, x, 1 - c)
    dev_x = [at(h, y, l, (x + d) % 4, c) for d in (1, 2, 3)]
    dev_l = [at(h, y, (l + d) % 4, x, c) for d in (1, 2, 3)]

    def remote(src, dst, s, r, dev):
        return pltpu.make_async_remote_copy(
            src_ref=src, dst_ref=dst, send_sem=s, recv_sem=r, device_id=dev, device_id_type=MESH
        )

    def token(tt):
        return (4 - tt) % 4

    def columns(hh, pp):
        return pl.ds(pl.multiple_of((hh * 2 + pp) * DP, DP), DP)

    def x_own(tt):
        rows = pl.ds(pl.multiple_of(token(tt) * TC, TC), TC)
        return pltpu.make_async_copy(x_hbm.at[rows, columns(h, pair)], xs.at[tt, 0, 0], sem_own.at[tt])

    def x_b(tt):
        rows = pl.ds(pl.multiple_of(token(tt) * TC + c * 64, 64), 64)
        return remote(
            x_hbm.at[rows, columns(h, 1 - pair)],
            xs.at[tt, 1, 0, pl.ds(pl.multiple_of(c * 64, 64), 64)],
            xb_s.at[tt], xb_r.at[tt], dev_b,
        )

    part = pl.ds(pl.multiple_of(c * 64 + x * 16, 16), 16)
    half = pl.ds(pl.multiple_of(c * 64, 64), 64)

    def x_z(tt):
        rows = pl.ds(pl.multiple_of(token(tt) * TC + c * 64 + x * 16, 16), 16)
        return remote(
            x_hbm.at[rows, columns(h2, pair)], xs.at[tt, 0, 1, part], xz_s.at[tt], xz_r.at[tt], dev_z
        )

    def x_d(tt):
        rows = pl.ds(pl.multiple_of(token(tt) * TC + c * 64 + x * 16, 16), 16)
        return remote(
            x_hbm.at[rows, columns(h2, 1 - pair)], xs.at[tt, 1, 1, part], xd_s.at[tt], xd_r.at[tt], dev_d
        )

    def x_x(tt, d):
        return remote(
            xs.at[tt, :, 1, part], xs.at[tt, :, 1, part], xx_s.at[tt, d], xx_r.at[tt, d], dev_x[d]
        )

    def x_c(tt):
        return remote(xs.at[tt, :, 1, half], xs.at[tt, :, 1, half], xc_s.at[tt], xc_r.at[tt], dev_c)

    def x_e(tt):
        return remote(xs.at[tt, 1, 0, half], xs.at[tt, 1, 0, half], xe_s.at[tt], xe_r.at[tt], dev_c)

    def w_rows():
        return pl.ds(pl.multiple_of(side * DB, DB), DB)

    def w_cols(f):
        return pl.ds(pl.multiple_of(f * FC, FC), FC)

    def w_own(f):
        return pltpu.make_async_copy(w_hbm.at[:, w_cols(f)], ws.at[f, w_rows()], sem_wo.at[f])

    def w_a(f):
        return remote(w_hbm.at[:, w_cols(f)], ws.at[f, w_rows()], w_s.at[f], w_r.at[f], dev_a)

    def hid_b(k):
        return remote(send_b.at[k], recv_b.at[k], b_s.at[k], b_r.at[k], dev_b)

    def hid_z(k):
        return remote(send_z.at[k], recv_z.at[k], z_s.at[k], z_r.at[k], dev_z)

    def grad_z(k):
        return remote(hg.at[k, 0, 0], hg.at[k, 0, 1], gz_s.at[k], gz_r.at[k], dev_z)

    def grad_0(k):
        return remote(hg.at[k, 0, 0], hg.at[k, 1, 0], g0_s.at[k], g0_r.at[k], dev_b)

    def grad_1(k):
        return remote(hg.at[k, 0, 1], hg.at[k, 1, 1], g1_s.at[k], g1_r.at[k], dev_b)

    def term_a(f):
        return remote(send_a.at[f], recv_a.at[f], a_s.at[f], a_r.at[f], dev_a)

    def gw_out(f):
        return pltpu.make_async_copy(gout.at[f], gw_hbm.at[:, w_cols(f)], sem_gw.at[f])

    def red_c(tt):
        return remote(send_c.at[tt], recv_c.at[tt], c_s.at[tt], c_r.at[tt], dev_c)

    def red_x(tt, d):
        return remote(send_x.at[tt, d], recv_x.at[tt, d], rx_s.at[tt, d], rx_r.at[tt, d], dev_x[d])

    def red_l(tt):
        root = token(tt)
        slot = (l - root + 4) % 4 - 1
        return remote(send_l.at[tt], recv_l.at[slot], l_s.at[tt], l_r.at[slot], at(h, y, root, x, c))

    def red_l_in(slot):
        return remote(send_l.at[0], recv_l.at[slot], l_s.at[0], l_r.at[slot], dev_l[0])

    mine = h * 2 + pair

    def final(n):
        return remote(send_f.at[n], fin.at[mine], f_s.at[n], f_r.at[n], (dev_z, dev_b, dev_d)[n])

    for tt in range(T):
        x_own(tt).start()
    for f in range(F):
        w_own(f).start()
    act_copy = pltpu.make_async_copy(act_hbm, act, sem_act)
    act_copy.start()

    barrier = pltpu.get_barrier_semaphore()
    everyone = [dev_a, dev_b, dev_z, dev_d, dev_c] + dev_x + dev_l
    for dev in everyone:
        pl.semaphore_signal(barrier, inc=1, device_id=dev, device_id_type=MESH)
    pl.semaphore_wait(barrier, len(everyone))

    w_a(0).start()
    for tt in range(2):
        x_z(tt).start()
        x_d(tt).start()
        x_b(tt).start()
    term[...] = jnp.zeros_like(term)
    for tt in range(T):
        x_own(tt).wait()
    for f in range(F):
        w_own(f).wait()
    act_copy.wait()

    def stage(step, offset, count, body):
        @pl.when((step >= offset) & (step < offset + count))
        def _():
            body(step - offset)

    def step_body(step, carry):
        def s4(k):
            hid_b(k).wait_recv()
            send_z[k] = (keep[k, 1] + recv_b[k, 1].astype(F32)).astype(BF16)
            hid_z(k).start()
            keep[k, 0] += recv_b[k, 0].astype(F32)

        stage(step, O_S4, K, s4)

        def s5(k):
            f, tt = k // T, k % T
            hid_z(k).wait_recv()
            hidden = keep[k, 0] + recv_z[k].astype(F32)
            rows = pl.ds(pl.multiple_of(token(tt) * TC, TC), TC)
            slope = gelu_slope(hidden)
            hg[k, 0, 0] = (act[rows, w_cols(f)].astype(F32) * slope).astype(BF16)
            grad_z(k).start()
            grad_0(k).start()

        stage(step, O_S5, K, s5)

        def s6(k):
            grad_z(k).wait_recv()
            grad_1(k).start()

        stage(step, O_S6, K, s6)

        def x1(tt):
            x_z(tt).wait_recv()
            x_d(tt).wait_recv()
            for d in range(3):
                x_x(tt, d).start()

            @pl.when(tt + 2 < T)
            def _():
                x_z(tt + 2).start()
                x_d(tt + 2).start()
                x_b(tt + 2).start()

        stage(step, O_X1, T, x1)

        def x2(tt):
            x_b(tt).wait_recv()
            x_e(tt).start()
            for d in range(3):
                x_x(tt, d).wait_recv()
            x_c(tt).start()

        stage(step, O_X2, T, x2)

        def s3(k):
            f, tt = k // T, k % T

            @pl.when(f == 0)
            def _():
                x_e(tt).wait_recv()
                x_c(tt).wait_recv()

            @pl.when(tt == 0)
            def _():
                w_a(f).wait_recv()

                @pl.when(f + 1 < F)
                def _():
                    w_a(f + 1).start()

            there = jnp.dot(
                xs[tt, 1].reshape(2 * TC, DP), ws[f], preferred_element_type=F32
            )
            send_b[k] = there.astype(BF16).reshape(2, TC, FC)
            hid_b(k).start()
            here = jnp.dot(
                xs[tt, 0].reshape(2 * TC, DP), ws[f], preferred_element_type=F32
            )
            keep[k] = here.reshape(2, TC, FC)

        stage(step, O_S3, K, s3)

        def s8(k):
            f, tt = k // T, k % T

            @pl.when(tt == T - 1)
            def _():
                term_a(f).wait_recv()
                own = pl.ds(pl.multiple_of(side * DB, DB), DB)
                total = (term[f, :, own] + recv_a[f].astype(F32)) * 0.125
                gout[f] = total.T
                gw_out(f).start()

        def r1(tt):
            red_c(tt).wait_recv()
            for d in range(4):
                xx = (x + d) % 4
                for blk in range(4):
                    rows = pl.ds(pl.multiple_of(blk * TC + xx * 32 + c * 16, 16), 16)
                    value = acc[rows, :] + recv_c[tt, xx, blk].astype(F32)
                    if d == 0:
                        keep_x[tt, blk] = value
                    else:
                        send_x[tt, d - 1, blk] = value.astype(BF16)
                if d:
                    red_x(tt, d - 1).start()

        stage(step, O_R1 + K - T, T, r1)

        def s7(k):
            f, tt = k // T, k % T
            grad_0(k).wait_recv()
            grad_1(k).wait_recv()
            grads = hg[k].reshape(4 * TC, FC)

            @pl.when(f == F - 1)
            def _():
                for j in range(DP // COLS):
                    cols = pl.ds(j * COLS, COLS)
                    acc[:, cols] = sum(
                        lax.dot_general(
                            hg[n * T + tt].reshape(4 * TC, FC), ws[n, cols, :],
                            (((1,), (1,)), ((), ())), preferred_element_type=F32,
                        )
                        for n in range(F)
                    )
                for xx in range(4):
                    for blk in range(4):
                        rows = pl.ds(pl.multiple_of(blk * TC + xx * 32 + (1 - c) * 16, 16), 16)
                        send_c[tt, xx, blk] = acc[rows, :].astype(BF16)
                red_c(tt).start()

            for j in range(DP // COLS):
                cols = pl.ds(j * COLS, COLS)
                term[f, :, cols] += lax.dot_general(
                    grads, xs[tt, :, :, :, cols].reshape(4 * TC, COLS),
                    (((0,), (0,)), ((), ())), preferred_element_type=F32,
                )

            @pl.when(tt == T - 1)
            def _():
                other = pl.ds(pl.multiple_of((1 - side) * DB, DB), DB)
                send_a[f] = term[f, :, other].astype(BF16)
                term_a(f).start()

        stage(step, O_S7, K, s7)
        stage(step, O_S8, K, s8)

        def r2(tt):
            for d in range(3):
                red_x(tt, d).wait_recv()
            value = keep_x[tt]
            for d in range(3):
                value = value + recv_x[tt, d].astype(F32)

            @pl.when(l == token(tt))
            def _():
                keep_l[...] = value

            @pl.when(l != token(tt))
            def _():
                send_l[tt] = value.astype(BF16)
                red_l(tt).start()

        stage(step, O_R2 + K - T, T, r2)

        def r3(tt):
            @pl.when(l == token(tt))
            def _():
                for slot in range(3):
                    red_l_in(slot).wait_recv()
                value = keep_l[...]
                for slot in range(3):
                    value = value + recv_l[slot].astype(F32)
                value = value.astype(BF16)
                fin[mine] = value[0]
                for n in range(3):
                    send_f[n] = value[n + 1]
                    final(n).start()

        stage(step, O_R3 + K - T, T, r3)
        return carry

    lax.fori_loop(0, STEPS, step_body, 0)

    for n in range(3):
        final(n).wait_recv()
    for n in range(4):
        ig_ref[:, n * DP : (n + 1) * DP] = fin[n]

    def drain_k(k, carry):
        for copy in (hid_b, hid_z, grad_z, grad_0, grad_1):
            copy(k).wait_send()
        return carry

    lax.fori_loop(0, K, drain_k, 0)

    def drain_t(tt, carry):
        for copy in (x_b, x_z, x_d, x_c, x_e, red_c):
            copy(tt).wait_send()
        for d in range(3):
            x_x(tt, d).wait_send()
            red_x(tt, d).wait_send()

        @pl.when(l != token(tt))
        def _():
            red_l(tt).wait_send()

        return carry

    lax.fori_loop(0, T, drain_t, 0)
    for f in range(F):
        w_a(f).wait_send()
        term_a(f).wait_send()
        gw_out(f).wait()
    for n in range(3):
        final(n).wait_send()


def scratch():
    dma = pltpu.SemaphoreType.DMA
    both = lambda *shape: [dma(shape), dma(shape)]
    return [
        pltpu.VMEM((T, 2, 2, TC, DP), BF16),
        pltpu.VMEM((F, DP, FC), BF16),
        pltpu.VMEM((512, 768), BF16),
        pltpu.VMEM((K, 2, TC, FC), BF16),
        pltpu.VMEM((K, 2, TC, FC), BF16),
        pltpu.VMEM((K, 2, TC, FC), F32),
        pltpu.VMEM((K, TC, FC), BF16),
        pltpu.VMEM((K, TC, FC), BF16),
        pltpu.VMEM((K, 2, 2, TC, FC), BF16),
        pltpu.VMEM((F, FC, DP), F32),
        pltpu.VMEM((4 * TC, DP), F32),
        pltpu.VMEM((T, 4, 4, 16, DP), BF16),
        pltpu.VMEM((T, 4, 4, 16, DP), BF16),
        pltpu.VMEM((T, 3, 4, 16, DP), BF16),
        pltpu.VMEM((T, 3, 4, 16, DP), BF16),
        pltpu.VMEM((T, 4, 16, DP), F32),
        pltpu.VMEM((T, 4, 16, DP), BF16),
        pltpu.VMEM((3, 4, 16, DP), BF16),
        pltpu.VMEM((4, 16, DP), F32),
        pltpu.VMEM((3, 16, DP), BF16),
        pltpu.VMEM((4, 16, DP), BF16),
        pltpu.VMEM((F, FC, DB), BF16),
        pltpu.VMEM((F, FC, DB), BF16),
        pltpu.VMEM((F, DB, FC), F32),
        dma((T,)), dma((F,)), dma, dma((F,)),
        *both(T), *both(T), *both(T), *both(T, 3), *both(T), *both(T),
        *both(F), *both(K), *both(K), *both(K), *both(K), *both(K),
        *both(F), *both(T), *both(T, 3),
        dma((T,)), dma((3,)), *both(3),
    ]


def dequant(codes, scales):
    return (codes.astype(F32) * scales.astype(F32)[:, None]).astype(BF16)


def local(inputs, act_grad, in_codes, in_scales):
    w_in = dequant(in_codes, in_scales)
    input_grad, in_grad = pl.pallas_call(
        kernel,
        out_shape=(
            jax.ShapeDtypeStruct((16, 6144), BF16),
            jax.ShapeDtypeStruct((768, 768), F32),
        ),
        in_specs=[pl.BlockSpec(memory_space=pl.ANY)] * 3,
        out_specs=(
            pl.BlockSpec(memory_space=pltpu.VMEM),
            pl.BlockSpec(memory_space=pl.ANY),
        ),
        scratch_shapes=scratch(),
        compiler_params=pltpu.CompilerParams(
            collective_id=0, has_side_effects=True, vmem_limit_bytes=60 * 1024 * 1024
        ),
        cost_estimate=pl.CostEstimate(
            flops=3 * 2 * 512 * 6144 * 768, bytes_accessed=12 * 1024 * 1024, transcendentals=512 * 768
        ),
        name="ffn_in_backward",
    )(inputs, act_grad, w_in)
    return input_grad, in_grad


def solution(mesh):
    return jax.shard_map(
        local,
        mesh=mesh,
        in_specs=(P("outer", None), P("outer", "inner"), P("outer", "inner"), P("outer")),
        out_specs=(P(("outer", "inner"), None), P("outer", "inner")),
        check_vma=False,
    )
```

```python
import functools

import jax
import jax.numpy as jnp
from jax import lax
from jax.experimental import pallas as pl
from jax.experimental.pallas import tpu as pltpu
from jax.sharding import PartitionSpec as P

coef = 0.7978845608
cubic = 0.044715

MESH = pl.DeviceIdType.MESH
F32 = jnp.float32
BF16 = jnp.bfloat16

F = 3
T = 8
K = T * F
FC = 256
TC = 64
DB = 768
DP = 1536
COLS = 256
OWN, ACROSS, DIAGONAL, BESIDE = 0, 1, 2, 3

O_S4, O_S5, O_S6, O_S7, O_R1, O_R2, O_R3, O_S8 = 3, 6, 9, 12, 13, 16, 2, 18
STEPS = K + O_R2 + 2 * O_R3


def chunk(n):
    late = n // 12
    r = n % 6
    second = r // 4 + (1 - r // 4) * (r % 2) * (1 - r // 2 % 2)
    t = (1 - late) * (n % 4) + late * (4 + 2 * ((n - 12 * late) // 6) + second)
    f = (1 - late) * (n // 4) + late * ((r + 2) // 4) * (r - 1 - 2 * (r // 4))
    return t, f


def gelu_slope(value):
    tangent = jnp.tanh(coef * (value + cubic * value * value * value))
    return 0.5 * (1.0 + tangent) + 0.5 * value * (1.0 - tangent * tangent) * coef * (
        1.0 + 3.0 * cubic * value * value
    )


def kernel(
    x_hbm, act_hbm, codes_hbm, scales_hbm, ig_ref, gw_hbm,
    xs, ws, codes, scales, act, send_b, recv_b, keep, send_z, recv_z, hg, term,
    acc, send_c, recv_c, send_x, recv_x, keep_x, send_l, recv_l,
    send_f, fin, send_a, recv_a, gout,
    sem_own, sem_in, sem_gw,
    xb_s, xb_r, xz_s, xz_r, xd_s, xd_r, xx_s, xx_r, xc_s, xc_r,
    w_s, w_r, b_s, b_r, z_s, z_r, gz_s, gz_r, g0_s, g0_r, g1_s, g1_r,
    a_s, a_r, c_s, c_r, rx_s, rx_r, l_s, l_r, f_s, f_r,
):
    o = lax.axis_index("outer")
    i = lax.axis_index("inner")
    h, y = o // 4, o % 4
    l, x, c = i // 8, (i // 2) % 4, i % 2
    pair, side = y // 2, y % 2
    h2, yb = 1 - h, 3 - y
    ya = pair * 2 + (1 - side)

    def at(hh, yy, ll, xx, cc):
        return (hh * 4 + yy, (ll * 4 + xx) * 2 + cc)

    dev_a = at(h, ya, l, x, c)
    dev_b = at(h, yb, l, x, c)
    dev_z = at(h2, y, l, x, c)
    dev_d = at(h2, yb, l, x, c)
    dev_c = at(h, y, l, x, 1 - c)
    dev_x = [at(h, y, l, (x + d) % 4, c) for d in (1, 2, 3)]
    dev_l = [at(h, y, (l + d) % 4, x, c) for d in (1, 2, 3)]

    barrier = pltpu.get_barrier_semaphore()
    everyone = [dev_a, dev_b, dev_z, dev_d, dev_c] + dev_x + dev_l
    for dev in everyone:
        pl.semaphore_signal(barrier, inc=1, device_id=dev, device_id_type=MESH)

    def remote(src, dst, s, r, dev):
        return pltpu.make_async_remote_copy(
            src_ref=src, dst_ref=dst, send_sem=s, recv_sem=r, device_id=dev, device_id_type=MESH
        )

    def root_l(t):
        return (4 - t // 2) % 4

    def root_c(t):
        return t % 2

    def columns(hh, pp):
        return pl.ds(pl.multiple_of((hh * 2 + pp) * DP, DP), DP)

    half = pl.ds(pl.multiple_of(c * DB, DB), DB)

    def half_columns(hh, pp):
        return pl.ds(pl.multiple_of((hh * 2 + pp) * DP + c * DB, DB), DB)

    def x_own(t):
        return pltpu.make_async_copy(
            x_hbm.at[root_l(t), :, root_c(t), :, columns(h, pair)], xs.at[t, OWN], sem_own.at[t]
        )

    def x_push(t, cols, block, s, r, dev):
        return remote(
            x_hbm.at[root_l(t), x, root_c(t), :, cols], xs.at[t, block, x, :, half], s.at[t], r.at[t], dev
        )

    def x_b(t):
        return x_push(t, half_columns(h, 1 - pair), BESIDE, xb_s, xb_r, dev_b)

    def x_z(t):
        return x_push(t, half_columns(h2, pair), ACROSS, xz_s, xz_r, dev_z)

    def x_d(t):
        return x_push(t, half_columns(h2, 1 - pair), DIAGONAL, xd_s, xd_r, dev_d)

    def x_x(t, d):
        part = xs.at[t, 1:4, x, :, half]
        return remote(part, part, xx_s.at[t, d], xx_r.at[t, d], dev_x[d])

    def x_c(t):
        part = xs.at[t, 1:4, :, :, half]
        return remote(part, part, xc_s.at[t], xc_r.at[t], dev_c)

    w_rows = pl.ds(pl.multiple_of(side * DB, DB), DB)

    def f_cols(f):
        return pl.ds(pl.multiple_of(f * FC, FC), FC)

    def w_a(f):
        part = ws.at[f, w_rows]
        return remote(part, part, w_s.at[f], w_r.at[f], dev_a)

    def hid_b(k):
        return remote(send_b.at[k], recv_b.at[k], b_s.at[k], b_r.at[k], dev_b)

    def hid_z(k):
        return remote(send_z.at[k], recv_z.at[k], z_s.at[k], z_r.at[k], dev_z)

    def grad_z(k):
        return remote(hg.at[k, OWN], hg.at[k, ACROSS], gz_s.at[k], gz_r.at[k], dev_z)

    def grad_0(k):
        return remote(hg.at[k, OWN], hg.at[k, BESIDE], g0_s.at[k], g0_r.at[k], dev_b)

    def grad_1(k):
        return remote(hg.at[k, ACROSS], hg.at[k, DIAGONAL], g1_s.at[k], g1_r.at[k], dev_b)

    def term_a(f):
        return remote(send_a.at[f], recv_a.at[f], a_s.at[f], a_r.at[f], dev_a)

    def gw_out(f):
        return pltpu.make_async_copy(gout.at[f], gw_hbm.at[:, f_cols(f)], sem_gw.at[f])

    def red_c(n):
        return remote(send_c.at[n], recv_c.at[n], c_s.at[n], c_r.at[n], dev_c)

    def red_x(n, d):
        return remote(send_x.at[n, d], recv_x.at[n, d], rx_s.at[n, d], rx_r.at[n, d], dev_x[d])

    def red_up(n):
        return remote(send_l.at[n], recv_l.at[n, 0], l_s.at[n], l_r.at[n, 0], at(h, y, (l + 1) % 4, x, c))

    def red_down(n):
        return remote(send_l.at[n], recv_l.at[n, 1], l_s.at[n], l_r.at[n, 1], at(h, y, (l + 3) % 4, x, c))

    def red_send(t):
        @pl.when(l < root_l(t))
        def _():
            red_up(t // 2).start()

        @pl.when(l > root_l(t))
        def _():
            red_down(t // 2).start()

    mine = h * 2 + pair

    def final(n):
        return remote(send_f.at[n], fin.at[mine], f_s.at[n], f_r.at[n], (dev_z, dev_d, dev_b)[n])

    codes_copy = pltpu.make_async_copy(codes_hbm, codes, sem_in.at[0])
    scales_copy = pltpu.make_async_copy(scales_hbm, scales, sem_in.at[1])
    act_copy = pltpu.make_async_copy(act_hbm, act, sem_in.at[2])
    scales_copy.start()
    codes_copy.start()
    for t in range(T):
        x_own(t).start()
    act_copy.start()
    scales_copy.wait()
    codes_copy.wait()
    scale = jnp.broadcast_to(scales[...].astype(F32).reshape(1, DB), (128, DB)).T
    for f in range(F):
        for j in range(FC // 128):
            value = codes[:, f * FC + j * 128 : f * FC + (j + 1) * 128].astype(F32) * scale
            ws[f, w_rows, j * 128 : (j + 1) * 128] = value.astype(BF16)

    pl.semaphore_wait(barrier, len(everyone))

    def x_start(t):
        x_d(t).start()
        x_z(t).start()
        x_b(t).start()

    def x_share(t):
        x_b(t).wait_recv()
        x_z(t).wait_recv()
        x_d(t).wait_recv()
        for d in range(3):
            x_x(t, d).start()

    def x_core(t):
        for d in range(3):
            x_x(t, d).wait_recv()
        x_c(t).start()

    x_start(0)
    w_a(0).start()
    x_start(1)
    w_a(1).start()
    x_start(2)
    w_a(2).start()
    for t in range(3, T):
        x_start(t)
    term[...] = jnp.zeros_like(term)
    x_share(0)
    act_copy.wait()
    x_share(1)
    x_core(0)
    x_share(2)
    x_core(1)

    def stage(step, offset, body):
        @pl.when((step >= offset) & (step < offset + K))
        def _():
            t, f = chunk(step - offset)
            body(t, f, t * F + f)

    def stage_t(step, offset, body):
        @pl.when((step >= offset) & (step < offset + K))
        def _():
            t, f = chunk(step - offset)

            @pl.when(f == F - 1)
            def _():
                body(t)

    def average(f):
        term_a(f).wait_recv()
        total = term[f, :, w_rows] + recv_a[f].astype(F32)
        gout[f] = total.T
        gw_out(f).start()

    def end(t):
        return ((l == 0) & (root_l(t) > 0)) | ((l == 3) & (root_l(t) < 3))

    def step_body(step, carry):
        def s4(t, f, k):
            hid_b(k).wait_recv()
            send_z[k] = (keep[k, 1] + recv_b[k, 0].astype(F32)).astype(BF16)
            hid_z(k).start()
            keep[k, 0] += recv_b[k, 1].astype(F32)

        stage(step, O_S4, s4)

        def s5(t, f, k):
            hid_z(k).wait_recv()
            hidden = keep[k, 0] + recv_z[k].astype(F32)
            given = act[root_l(t), :, root_c(t), :, f_cols(f)].reshape(TC, FC)
            hg[k, OWN] = (given.astype(F32) * gelu_slope(hidden)).astype(BF16)
            grad_z(k).start()
            grad_0(k).start()

        stage(step, O_S5, s5)

        def s6(t, f, k):
            grad_z(k).wait_recv()
            grad_1(k).start()

        stage(step, O_S6, s6)

        @pl.when(step == 0)
        def _():
            x_share(3)

        @pl.when(step < 2)
        def _():
            x_core(step + 2)

        @pl.when((step % 2 == 0) & (step >= 4) & (step <= 10))
        def _():
            x_share((step + 4) // 2)

        @pl.when((step % 2 == 0) & (step >= 6) & (step <= 12))
        def _():
            x_core((step + 2) // 2)

        def s3(t, f, k):

            @pl.when(f == 0)
            def _():
                x_own(t).wait()
                x_c(t).wait_recv()

            @pl.when(t == 0)
            def _():
                w_a(f).wait_recv()

            both = jnp.dot(xs[t].reshape(4 * TC, DP), ws[f], preferred_element_type=F32)
            send_b[k] = both[2 * TC :].astype(BF16).reshape(2, TC, FC)
            hid_b(k).start()
            keep[k] = both[: 2 * TC].reshape(2, TC, FC)

        stage(step, 0, s3)

        def s7(t, f, k):
            grad_0(k).wait_recv()
            grad_1(k).wait_recv()
            grads = hg[k].reshape(4 * TC, FC)

            def partial(cols):
                return sum(
                    lax.dot_general(
                        hg[t * F + n].reshape(4 * TC, FC), ws[n, cols, :],
                        (((1,), (1,)), ((), ())), preferred_element_type=F32,
                    )
                    for n in range(F)
                )

            @pl.when((f == F - 1) & (c == root_c(t)))
            def _():
                for j in range(DP // COLS):
                    cols = pl.ds(j * COLS, COLS)
                    acc[t // 2, :, cols] = partial(cols)

            @pl.when((f == F - 1) & (c != root_c(t)))
            def _():
                for j in range(DP // COLS):
                    cols = pl.ds(j * COLS, COLS)
                    send_c[t // 2, :, cols] = partial(cols).astype(BF16)
                red_c(t // 2).start()

            for j in range(DP // COLS):
                cols = pl.ds(j * COLS, COLS)
                term[f, :, cols] += lax.dot_general(
                    grads, xs[t, :, :, :, cols].reshape(4 * TC, COLS),
                    (((0,), (0,)), ((), ())), preferred_element_type=F32,
                )

            @pl.when(t == T - 1)
            def _():
                other = pl.ds(pl.multiple_of((1 - side) * DB, DB), DB)
                send_a[f] = term[f, :, other].astype(BF16)
                term_a(f).start()

        stage(step, O_S7, s7)

        def r1(t):
            n = t // 2

            @pl.when(c == root_c(t))
            def _():
                red_c(n).wait_recv()
                for d in (1, 2, 3, 0):
                    xx = (x + d) % 4
                    for block in range(4):
                        rows = pl.ds(pl.multiple_of(block * TC + xx * 16, 16), 16)
                        value = acc[n, rows, :] + recv_c[n, rows, :].astype(F32)
                        if d == 0:
                            keep_x[n, block] = value
                        else:
                            send_x[n, d - 1, block] = value.astype(BF16)
                    if d:
                        red_x(n, d - 1).start()

        stage_t(step, O_R1, r1)

        def r2(t):
            n = t // 2

            @pl.when(c == root_c(t))
            def _():
                for d in range(3):
                    red_x(n, d).wait_recv()
                value = keep_x[n]
                for d in range(3):
                    value = value + recv_x[n, d].astype(F32)

                keep_x[n] = value

                @pl.when(end(t))
                def _():
                    send_l[n] = value.astype(BF16)
                    red_send(t)

        stage_t(step, O_R2, r2)

        for depth in (1, 2):

            def r3(t):
                n = t // 2

                @pl.when((c == root_c(t)) & (l < root_l(t)) & (l == depth))
                def _():
                    red_up(n).wait_recv()
                    send_l[n] = (keep_x[n] + recv_l[n, 0].astype(F32)).astype(BF16)
                    red_up(n).start()

                @pl.when((c == root_c(t)) & (l > root_l(t)) & (3 - l == depth))
                def _():
                    red_down(n).wait_recv()
                    send_l[n] = (keep_x[n] + recv_l[n, 1].astype(F32)).astype(BF16)
                    red_down(n).start()

            stage_t(step, O_R2 + O_R3 * depth, r3)

        def s8(t, f, k):
            @pl.when((t == T - 1) & (f < F - 1))
            def _():
                average(f)

        stage(step, O_S8, s8)
        return carry

    lax.fori_loop(0, STEPS, step_body, 0)

    last = (4 - l) % 4

    @pl.when(l > 0)
    def _():
        red_up(last).wait_recv()
        keep_x[last] += recv_l[last, 0].astype(F32)

    @pl.when(l < 3)
    def _():
        red_down(last).wait_recv()
        keep_x[last] += recv_l[last, 1].astype(F32)

    value = keep_x[last]
    value = value.astype(BF16)
    fin[mine] = value[OWN]
    for n in range(3):
        send_f[n] = value[n + 1]
        final(n).start()

    average(F - 1)

    def drain_k(k, carry):
        for copy in (hid_b, hid_z, grad_z, grad_0, grad_1):
            copy(k).wait_send()
        return carry

    lax.fori_loop(0, K, drain_k, 0)

    def drain_t(t, carry):
        n = t // 2
        for copy in (x_b, x_z, x_d, x_c):
            copy(t).wait_send()
        for d in range(3):
            x_x(t, d).wait_send()

        @pl.when(c != root_c(t))
        def _():
            red_c(n).wait_send()

        @pl.when(c == root_c(t))
        def _():
            for d in range(3):
                red_x(n, d).wait_send()

            @pl.when(l != root_l(t))
            def _():
                red_up(n).wait_send()

        return carry

    lax.fori_loop(0, T, drain_t, 0)
    for f in range(F):
        w_a(f).wait_send()
        term_a(f).wait_send()

    for n in range(3):
        final(n).wait_recv()
    for n in range(4):
        ig_ref[:, n * DP : (n + 1) * DP] = fin[n]
    for f in range(F):
        gw_out(f).wait()
    for n in range(3):
        final(n).wait_send()


def scratch():
    dma = pltpu.SemaphoreType.DMA
    both = lambda *shape: [dma(shape), dma(shape)]
    H = T // 2
    return [
        pltpu.VMEM((T, 4, 4, 16, DP), BF16),
        pltpu.VMEM((F, DP, FC), BF16),
        pltpu.VMEM((DB, 768), BF16),
        pltpu.VMEM((DB,), BF16),
        pltpu.VMEM((4, 4, 2, 16, 768), BF16),
        pltpu.VMEM((K, 2, TC, FC), BF16),
        pltpu.VMEM((K, 2, TC, FC), BF16),
        pltpu.VMEM((K, 2, TC, FC), F32),
        pltpu.VMEM((K, TC, FC), BF16),
        pltpu.VMEM((K, TC, FC), BF16),
        pltpu.VMEM((K, 4, TC, FC), BF16),
        pltpu.VMEM((F, FC, DP), F32),
        pltpu.VMEM((H, 4 * TC, DP), F32),
        pltpu.VMEM((H, 4 * TC, DP), BF16),
        pltpu.VMEM((H, 4 * TC, DP), BF16),
        pltpu.VMEM((H, 3, 4, 16, DP), BF16),
        pltpu.VMEM((H, 3, 4, 16, DP), BF16),
        pltpu.VMEM((H, 4, 16, DP), F32),
        pltpu.VMEM((H, 4, 16, DP), BF16),
        pltpu.VMEM((H, 2, 4, 16, DP), BF16),
        pltpu.VMEM((3, 16, DP), BF16),
        pltpu.VMEM((4, 16, DP), BF16),
        pltpu.VMEM((F, FC, DB), BF16),
        pltpu.VMEM((F, FC, DB), BF16),
        pltpu.VMEM((F, DB, FC), F32),
        dma((T,)), dma((3,)), dma((F,)),
        *both(T), *both(T), *both(T), *both(T, 3), *both(T),
        *both(F), *both(K), *both(K), *both(K), *both(K), *both(K),
        *both(F), *both(H), *both(H, 3),
        dma((H,)), dma((H, 2)), *both(3),
    ]


def local(inputs, act_grad, in_codes, in_scales):
    input_grad, in_grad = pl.pallas_call(
        kernel,
        out_shape=(
            jax.ShapeDtypeStruct((16, 6144), BF16),
            jax.ShapeDtypeStruct((768, 768), F32),
        ),
        in_specs=[pl.BlockSpec(memory_space=pl.ANY)] * 4,
        out_specs=(
            pl.BlockSpec(memory_space=pltpu.VMEM),
            pl.BlockSpec(memory_space=pl.ANY),
        ),
        scratch_shapes=scratch(),
        compiler_params=pltpu.CompilerParams(
            collective_id=0, has_side_effects=True, vmem_limit_bytes=60 * 1024 * 1024
        ),
        cost_estimate=pl.CostEstimate(
            flops=3 * 2 * 512 * 6144 * 768, bytes_accessed=12 * 1024 * 1024, transcendentals=512 * 768
        ),
        name="ffn_in_backward",
    )(
        inputs.reshape(4, 4, 2, 16, 6144),
        act_grad.reshape(4, 4, 2, 16, 768),
        in_codes,
        in_scales,
    )
    return input_grad, in_grad * 0.125


def solution(mesh):
    return jax.shard_map(
        local,
        mesh=mesh,
        in_specs=(P("outer", None), P("outer", "inner"), P("outer", "inner"), P("outer")),
        out_specs=(P(("outer", "inner"), None), P("outer", "inner")),
        check_vma=False,
    )
```

```python
import functools

import jax
import jax.numpy as jnp
from jax import lax
from jax.experimental import pallas as pl
from jax.experimental.pallas import tpu as pltpu
from jax.sharding import PartitionSpec as P

coef = 0.7978845608
cubic = 0.044715

MESH = pl.DeviceIdType.MESH
F32 = jnp.float32
BF16 = jnp.bfloat16

F = 3
T = 8
K = T * F
FC = 256
TC = 64
DB = 768
DP = 1536
COLS = 256
OWN, ACROSS, DIAGONAL, BESIDE = 0, 1, 2, 3

O_S4, O_S5, O_S6, O_S7, O_R1, O_R2, O_R3 = 3, 6, 9, 12, 13, 19, 3
STEPS = K + O_R2 + 2 * O_R3


def chunk(n):
    late = n // 12
    r = n % 6
    second = r // 4 + (1 - r // 4) * (r % 2) * (1 - r // 2 % 2)
    t = (1 - late) * (n % 4) + late * (4 + 2 * ((n - 12 * late) // 6) + second)
    f = (1 - late) * (n // 4) + late * ((r + 2) // 4) * (r - 1 - 2 * (r // 4))
    return t, f


def gelu_slope(value):
    tangent = jnp.tanh(coef * (value + cubic * value * value * value))
    return 0.5 * (1.0 + tangent) + 0.5 * value * (1.0 - tangent * tangent) * coef * (
        1.0 + 3.0 * cubic * value * value
    )


def kernel(
    x_hbm, act_hbm, codes_hbm, scales_hbm, ig_hbm, gw_hbm,
    xs, ws, codes, scales, act, send_b, recv_b, keep, send_z, recv_z, hg, term,
    acc, send_c, recv_c, send_x, recv_x, keep_x, send_l, recv_l,
    send_f, fin, send_a, recv_a, gout,
    sem_own, sem_in, sem_gw, sem_ig,
    xb_s, xz_s, xd_s, xp_r, xx_s, xx_r, xc_s, xc_r,
    w_s, w_r, b_s, b_r, z_s, z_r, gz_s, gz_r, g0_s, g1_s, g_r,
    a_s, a_r, c_s, c_r, rx_s, rx_r, l_s, l_r, f_s, f_r,
):
    o = lax.axis_index("outer")
    i = lax.axis_index("inner")
    h, y = o // 4, o % 4
    l, x, c = i // 8, (i // 2) % 4, i % 2
    pair, side = y // 2, y % 2
    h2, yb = 1 - h, 3 - y
    ya = pair * 2 + (1 - side)

    def at(hh, yy, ll, xx, cc):
        return (hh * 4 + yy, (ll * 4 + xx) * 2 + cc)

    dev_a = at(h, ya, l, x, c)
    dev_b = at(h, yb, l, x, c)
    dev_z = at(h2, y, l, x, c)
    dev_d = at(h2, yb, l, x, c)
    dev_c = at(h, y, l, x, 1 - c)
    dev_x = [at(h, y, l, (x + d) % 4, c) for d in (1, 2, 3)]
    dev_l = [at(h, y, (l + d) % 4, x, c) for d in (1, 2, 3)]

    barrier = pltpu.get_barrier_semaphore()
    everyone = [dev_a, dev_b, dev_z, dev_d, dev_c] + dev_x + dev_l
    for dev in everyone:
        pl.semaphore_signal(barrier, inc=1, device_id=dev, device_id_type=MESH)

    def remote(src, dst, s, r, dev):
        return pltpu.make_async_remote_copy(
            src_ref=src, dst_ref=dst, send_sem=s, recv_sem=r, device_id=dev, device_id_type=MESH
        )

    def root_l(t):
        return (4 - t // 2) % 4

    def root_c(t):
        return t % 2

    def columns(hh, pp):
        return pl.ds(pl.multiple_of((hh * 2 + pp) * DP, DP), DP)

    half = pl.ds(pl.multiple_of(c * DB, DB), DB)

    def half_columns(hh, pp):
        return pl.ds(pl.multiple_of((hh * 2 + pp) * DP + c * DB, DB), DB)

    def x_own(t):
        return pltpu.make_async_copy(
            x_hbm.at[root_l(t), :, root_c(t), :, columns(h, pair)], xs.at[t, OWN], sem_own
        )

    def x_push(t, cols, block, s, dev):
        return remote(
            x_hbm.at[root_l(t), x, root_c(t), :, cols], xs.at[t, block, x, :, half], s, xp_r.at[t], dev
        )

    def x_b(t):
        return x_push(t, half_columns(h, 1 - pair), BESIDE, xb_s, dev_b)

    def x_z(t):
        return x_push(t, half_columns(h2, pair), ACROSS, xz_s, dev_z)

    def x_d(t):
        return x_push(t, half_columns(h2, 1 - pair), DIAGONAL, xd_s, dev_d)

    def x_x(t, d):
        part = xs.at[t, 1:4, x, :, half]
        return remote(part, part, xx_s.at[d], xx_r.at[t], dev_x[d])

    def x_c(t):
        part = xs.at[t, 1:4, :, :, half]
        return remote(part, part, xc_s, xc_r.at[t], dev_c)

    w_rows = pl.ds(pl.multiple_of(side * DB, DB), DB)

    def f_cols(f):
        return pl.ds(pl.multiple_of(f * FC, FC), FC)

    def w_a(f):
        part = ws.at[f, w_rows]
        return remote(part, part, w_s, w_r.at[f], dev_a)

    def hid_b(k):
        return remote(send_b.at[k], recv_b.at[k], b_s, b_r.at[k], dev_b)

    def hid_z(k):
        return remote(send_z.at[k], recv_z.at[k], z_s, z_r.at[k], dev_z)

    def grad_z(k):
        return remote(hg.at[k, OWN], hg.at[k, ACROSS], gz_s, gz_r.at[k], dev_z)

    def grad_0(k):
        return remote(hg.at[k, OWN], hg.at[k, BESIDE], g0_s, g_r.at[k], dev_b)

    def grad_1(k):
        return remote(hg.at[k, ACROSS], hg.at[k, DIAGONAL], g1_s, g_r.at[k], dev_b)

    def term_a(f):
        return remote(send_a.at[f], recv_a.at[f], a_s, a_r.at[f], dev_a)

    def gw_out(f):
        return pltpu.make_async_copy(gout.at[f], gw_hbm.at[:, f_cols(f)], sem_gw)

    def red_c(n):
        return remote(send_c.at[n], recv_c.at[n], c_s, c_r.at[n], dev_c)

    def red_x(n, d):
        return remote(send_x.at[n, d], recv_x.at[n, d], rx_s.at[d], rx_r.at[n], dev_x[d])

    def red_up(n):
        return remote(send_l.at[n], recv_l.at[n, 0], l_s, l_r.at[n, 0], at(h, y, (l + 1) % 4, x, c))

    def red_down(n):
        return remote(send_l.at[n], recv_l.at[n, 1], l_s, l_r.at[n, 1], at(h, y, (l + 3) % 4, x, c))

    def red_send(t):
        @pl.when(l < root_l(t))
        def _():
            red_up(t // 2).start()

        @pl.when(l > root_l(t))
        def _():
            red_down(t // 2).start()

    mine = h * 2 + pair

    def final(n):
        return remote(send_f.at[n], fin.at[mine], f_s, f_r, (dev_z, dev_d, dev_b)[n])

    def ig_out(n):
        return pltpu.make_async_copy(fin.at[n], ig_hbm.at[:, n * DP : (n + 1) * DP], sem_ig)

    codes_copy = pltpu.make_async_copy(codes_hbm, codes, sem_in.at[0])
    scales_copy = pltpu.make_async_copy(scales_hbm, scales, sem_in.at[1])
    act_copy = pltpu.make_async_copy(act_hbm, act, sem_in.at[2])
    scales_copy.start()
    codes_copy.start()
    for t in range(T):
        x_own(t).start()
    act_copy.start()
    scales_copy.wait()
    codes_copy.wait()
    scale = jnp.broadcast_to(scales[...].astype(F32).reshape(1, DB), (128, DB)).T
    for f in range(F):
        for j in range(FC // 128):
            value = codes[:, f * FC + j * 128 : f * FC + (j + 1) * 128].astype(F32) * scale
            ws[f, w_rows, j * 128 : (j + 1) * 128] = value.astype(BF16)

    pl.semaphore_wait(barrier, len(everyone))

    def x_start(t):
        x_d(t).start()
        x_z(t).start()
        x_b(t).start()

    def x_share(t):
        part = xs.at[t, 1:4, x, :, half]
        remote(part, part, xc_s, xp_r.at[t], dev_c).wait_recv()
        for d in range(3):
            x_x(t, d).start()

    def x_core(t):
        part = xs.at[t, 1:4, 0:3, :, half]
        remote(part, part, xc_s, xx_r.at[t], dev_c).wait_recv()
        x_c(t).start()

    x_start(0)
    w_a(0).start()
    x_start(1)
    w_a(1).start()
    x_start(2)
    w_a(2).start()
    for t in range(3, T):
        x_start(t)
    term[...] = jnp.zeros_like(term)
    x_share(0)
    act_copy.wait()
    pltpu.make_async_copy(xs.at[:, OWN], xs.at[:, OWN], sem_own).wait()
    x_share(1)
    x_core(0)
    x_share(2)
    x_core(1)

    def stage(step, offset, body):
        @pl.when((step >= offset) & (step < offset + K))
        def _():
            t, f = chunk(step - offset)
            body(t, f, t * F + f)

    def stage_t(step, offset, body):
        @pl.when((step >= offset) & (step < offset + K))
        def _():
            t, f = chunk(step - offset)

            @pl.when(f == F - 1)
            def _():
                body(t)

    def average(f):
        term_a(f).wait_recv()
        total = term[f, :, w_rows] + recv_a[f].astype(F32)
        gout[f] = total.T
        gw_out(f).start()

    def end(t):
        return ((l == 0) & (root_l(t) > 0)) | ((l == 3) & (root_l(t) < 3))

    def step_body(step, carry):
        def s4(t, f, k):
            hid_b(k).wait_recv()
            send_z[k] = (keep[k, 1] + recv_b[k, 0].astype(F32)).astype(BF16)
            hid_z(k).start()
            keep[k, 0] += recv_b[k, 1].astype(F32)

        stage(step, O_S4, s4)

        def s5(t, f, k):
            hid_z(k).wait_recv()
            hidden = keep[k, 0] + recv_z[k].astype(F32)
            given = act[root_l(t), :, root_c(t), :, f_cols(f)].reshape(TC, FC)
            hg[k, OWN] = (given.astype(F32) * gelu_slope(hidden)).astype(BF16)
            grad_z(k).start()
            grad_0(k).start()

        stage(step, O_S5, s5)

        def s6(t, f, k):
            grad_z(k).wait_recv()
            grad_1(k).start()

        stage(step, O_S6, s6)

        def s3(t, f, k):

            @pl.when(f == 0)
            def _():
                x_c(t).wait_recv()

            @pl.when(t == 0)
            def _():
                w_a(f).wait_recv()

            both = jnp.dot(xs[t].reshape(4 * TC, DP), ws[f], preferred_element_type=F32)
            send_b[k] = both[2 * TC :].astype(BF16).reshape(2, TC, FC)
            hid_b(k).start()
            keep[k] = both[: 2 * TC].reshape(2, TC, FC)

        stage(step, 0, s3)

        @pl.when(step == 0)
        def _():
            x_share(3)

        @pl.when(step < 2)
        def _():
            x_core(step + 2)

        @pl.when((step % 2 == 0) & (step >= 4) & (step <= 10))
        def _():
            x_share((step + 4) // 2)

        @pl.when((step % 2 == 0) & (step >= 6) & (step <= 12))
        def _():
            x_core((step + 2) // 2)

        def s7(t, f, k):
            beside = hg.at[k, 2:4]
            remote(beside, beside, g0_s, g_r.at[k], dev_b).wait_recv()
            grads = hg[k].reshape(4 * TC, FC)

            def partial(cols):
                return sum(
                    lax.dot_general(
                        hg[t * F + n].reshape(4 * TC, FC), ws[n, cols, :],
                        (((1,), (1,)), ((), ())), preferred_element_type=F32,
                    )
                    for n in range(F)
                )

            @pl.when((f == F - 1) & (c == root_c(t)))
            def _():
                for j in range(DP // COLS):
                    cols = pl.ds(j * COLS, COLS)
                    acc[t // 2, :, cols] = partial(cols)

            @pl.when((f == F - 1) & (c != root_c(t)))
            def _():
                for j in range(DP // COLS):
                    cols = pl.ds(j * COLS, COLS)
                    send_c[t // 2, :, cols] = partial(cols).astype(BF16)
                red_c(t // 2).start()

            for j in range(DP // COLS):
                cols = pl.ds(j * COLS, COLS)
                term[f, :, cols] += lax.dot_general(
                    grads, xs[t, :, :, :, cols].reshape(4 * TC, COLS),
                    (((0,), (0,)), ((), ())), preferred_element_type=F32,
                )

            @pl.when(t == T - 1)
            def _():
                other = pl.ds(pl.multiple_of((1 - side) * DB, DB), DB)
                send_a[f] = term[f, :, other].astype(BF16)
                term_a(f).start()

        stage(step, O_S7, s7)

        def r1(t):
            n = t // 2

            @pl.when(c == root_c(t))
            def _():
                red_c(n).wait_recv()
                for d in (1, 2, 3, 0):
                    xx = (x + d) % 4
                    for block in range(4):
                        rows = pl.ds(pl.multiple_of(block * TC + xx * 16, 16), 16)
                        value = acc[n, rows, :] + recv_c[n, rows, :].astype(F32)
                        if d == 0:
                            keep_x[n, block] = value
                        else:
                            send_x[n, d - 1, block] = value.astype(BF16)
                    if d:
                        red_x(n, d - 1).start()

        stage_t(step, O_R1, r1)

        def r2(t):
            n = t // 2

            @pl.when(c == root_c(t))
            def _():
                remote(send_x.at[n], recv_x.at[n], rx_s.at[0], rx_r.at[n], dev_c).wait_recv()
                value = keep_x[n]
                for d in range(3):
                    value = value + recv_x[n, d].astype(F32)

                keep_x[n] = value

                @pl.when(end(t))
                def _():
                    send_l[n] = value.astype(BF16)
                    red_send(t)

        stage_t(step, O_R2, r2)

        for depth in (1, 2):

            def r3(t):
                n = t // 2

                @pl.when((c == root_c(t)) & (l < root_l(t)) & (l == depth))
                def _():
                    red_up(n).wait_recv()
                    send_l[n] = (keep_x[n] + recv_l[n, 0].astype(F32)).astype(BF16)
                    red_up(n).start()

                @pl.when((c == root_c(t)) & (l > root_l(t)) & (3 - l == depth))
                def _():
                    red_down(n).wait_recv()
                    send_l[n] = (keep_x[n] + recv_l[n, 1].astype(F32)).astype(BF16)
                    red_down(n).start()

            stage_t(step, O_R2 + O_R3 * depth, r3)

        return carry

    lax.fori_loop(0, STEPS, step_body, 0)

    for f in range(F - 1):
        average(f)

    last = (4 - l) % 4

    @pl.when(l > 0)
    def _():
        red_up(last).wait_recv()
        keep_x[last] += recv_l[last, 0].astype(F32)

    @pl.when(l < 3)
    def _():
        red_down(last).wait_recv()
        keep_x[last] += recv_l[last, 1].astype(F32)

    value = keep_x[last]
    value = value.astype(BF16)
    fin[mine] = value[OWN]
    for n in range(3):
        send_f[n] = value[n + 1]
        final(n).start()

    average(F - 1)

    def left(buffer, s):
        remote(buffer, buffer, s, f_r, dev_c).wait_send()

    pushed = xs.at[:, BESIDE, x, :, half]
    for s in (xb_s, xz_s, xd_s):
        left(pushed, s)
    for d in range(3):
        left(xs.at[:, 1:4, x, :, half], xx_s.at[d])
        left(send_x.at[:, d], rx_s.at[d])
    left(xs.at[:, 1:4, :, :, half], xc_s)
    left(ws.at[:, w_rows], w_s)
    left(send_b, b_s)
    left(send_z, z_s)
    left(hg.at[:, OWN], gz_s)
    left(hg.at[:, OWN], g0_s)
    left(hg.at[:, ACROSS], g1_s)
    left(send_a, a_s)
    left(send_c, c_s)
    left(send_l.at[0:3], l_s)
    left(send_f, f_s)

    remote(fin.at[0:3], fin.at[0:3], f_s, f_r, dev_c).wait_recv()
    for n in range(4):
        ig_out(n).start()
    pltpu.make_async_copy(gout, gout, sem_gw).wait()
    pltpu.make_async_copy(fin, fin, sem_ig).wait()


def scratch():
    dma = pltpu.SemaphoreType.DMA
    H = T // 2
    return [
        pltpu.VMEM((T, 4, 4, 16, DP), BF16),
        pltpu.VMEM((F, DP, FC), BF16),
        pltpu.VMEM((DB, 768), BF16),
        pltpu.VMEM((DB,), BF16),
        pltpu.VMEM((4, 4, 2, 16, 768), BF16),
        pltpu.VMEM((K, 2, TC, FC), BF16),
        pltpu.VMEM((K, 2, TC, FC), BF16),
        pltpu.VMEM((K, 2, TC, FC), F32),
        pltpu.VMEM((K, TC, FC), BF16),
        pltpu.VMEM((K, TC, FC), BF16),
        pltpu.VMEM((K, 4, TC, FC), BF16),
        pltpu.VMEM((F, FC, DP), F32),
        pltpu.VMEM((H, 4 * TC, DP), F32),
        pltpu.VMEM((H, 4 * TC, DP), BF16),
        pltpu.VMEM((H, 4 * TC, DP), BF16),
        pltpu.VMEM((H, 3, 4, 16, DP), BF16),
        pltpu.VMEM((H, 3, 4, 16, DP), BF16),
        pltpu.VMEM((H, 4, 16, DP), F32),
        pltpu.VMEM((H, 4, 16, DP), BF16),
        pltpu.VMEM((H, 2, 4, 16, DP), BF16),
        pltpu.VMEM((3, 16, DP), BF16),
        pltpu.VMEM((4, 16, DP), BF16),
        pltpu.VMEM((F, FC, DB), BF16),
        pltpu.VMEM((F, FC, DB), BF16),
        pltpu.VMEM((F, DB, FC), F32),
        dma, dma((3,)), dma, dma,
        dma, dma, dma, dma((T,)), dma((3,)), dma((T,)), dma, dma((T,)),
        dma, dma((F,)), dma, dma((K,)), dma, dma((K,)), dma, dma((K,)), dma, dma, dma((K,)),
        dma, dma((F,)), dma, dma((H,)), dma((3,)), dma((H,)), dma, dma((H, 2)), dma, dma,
    ]


def local(inputs, act_grad, in_codes, in_scales):
    input_grad, in_grad = pl.pallas_call(
        kernel,
        out_shape=(
            jax.ShapeDtypeStruct((16, 6144), BF16),
            jax.ShapeDtypeStruct((768, 768), F32),
        ),
        in_specs=[pl.BlockSpec(memory_space=pl.ANY)] * 4,
        out_specs=(
            pl.BlockSpec(memory_space=pl.ANY),
            pl.BlockSpec(memory_space=pl.ANY),
        ),
        scratch_shapes=scratch(),
        compiler_params=pltpu.CompilerParams(
            collective_id=0, has_side_effects=True, vmem_limit_bytes=60 * 1024 * 1024
        ),
        cost_estimate=pl.CostEstimate(
            flops=3 * 2 * 512 * 6144 * 768, bytes_accessed=12 * 1024 * 1024, transcendentals=512 * 768
        ),
        name="ffn_in_backward",
    )(
        inputs.reshape(4, 4, 2, 16, 6144),
        act_grad.reshape(4, 4, 2, 16, 768),
        in_codes,
        in_scales,
    )
    return input_grad, in_grad * 0.125


def solution(mesh):
    return jax.shard_map(
        local,
        mesh=mesh,
        in_specs=(P("outer", None), P("outer", "inner"), P("outer", "inner"), P("outer")),
        out_specs=(P(("outer", "inner"), None), P("outer", "inner")),
        check_vma=False,
    )
```

```python
import functools

import jax
import jax.numpy as jnp
from jax import lax
from jax.experimental import pallas as pl
from jax.experimental.pallas import tpu as pltpu
from jax.sharding import PartitionSpec as P

coef = 0.7978845608
cubic = 0.044715

MESH = pl.DeviceIdType.MESH
F32 = jnp.float32
BF16 = jnp.bfloat16

F = 3
H = 4
T = 2 * H
K = T * F
FC = 256
TC = 64
DB = 768
DP = 1536
COLS = 256
OWN, ACROSS, DIAGONAL, BESIDE = 0, 1, 2, 3

O_S4, O_S5, O_S6, O_S7, O_R1, O_R2, O_R3 = 3, 6, 9, 12, 13, 19, 3
STEPS = K + O_R2 + 2 * O_R3


def chunk(n):
    late = n // 12
    r = n % 6
    second = r // 4 + (1 - r // 4) * (r % 2) * (1 - r // 2 % 2)
    t = (1 - late) * (n % 4) + late * (4 + 2 * ((n - 12 * late) // 6) + second)
    f = (1 - late) * (n // 4) + late * ((r + 2) // 4) * (r - 1 - 2 * (r // 4))
    return t, f


def gelu_slope(value):
    tangent = jnp.tanh(coef * (value + cubic * value * value * value))
    return 0.5 * (1.0 + tangent) + 0.5 * value * (1.0 - tangent * tangent) * coef * (
        1.0 + 3.0 * cubic * value * value
    )


def kernel(
    x_hbm, act_hbm, codes_hbm, scales_hbm, ig_hbm, gw_hbm,
    xs, ws, codes, scales, act, send_b, recv_b, keep, send_z, recv_z, hg, term,
    acc, send_c, recv_c, send_x, recv_x, keep_x, send_l, recv_l, recv_f,
    send_f, fin, send_a, recv_a, gout,
    sem_own, sem_in, sem_gw, sem_ig,
    xb_s, xz_s, xd_s, xp_r, xx_s, xx_r, xc_s, xc_r,
    w_s, w_r, b_s, b_r, z_s, z_r, gz_s, gz_r, g0_s, g1_s, g_r,
    a_s, a_r, c_s, c_r, rx_s, rx_r, l_s, l_r, lf_r, f_s, f_r,
):
    o = lax.axis_index("outer")
    i = lax.axis_index("inner")
    h, y = o // 4, o % 4
    l, x, c = i // 8, (i // 2) % 4, i % 2
    pair, side = y // 2, y % 2
    h2, yb = 1 - h, 3 - y
    ya = pair * 2 + (1 - side)

    def at(hh, yy, ll, xx, cc):
        return (hh * 4 + yy, (ll * 4 + xx) * 2 + cc)

    dev_a = at(h, ya, l, x, c)
    dev_b = at(h, yb, l, x, c)
    dev_z = at(h2, y, l, x, c)
    dev_d = at(h2, yb, l, x, c)
    dev_c = at(h, y, l, x, 1 - c)
    dev_x = [at(h, y, l, (x + d) % 4, c) for d in (1, 2, 3)]
    dev_l = [at(h, y, (l + d) % 4, x, c) for d in (1, 2, 3)]

    barrier = pltpu.get_barrier_semaphore()
    everyone = [dev_a, dev_b, dev_z, dev_d, dev_c] + dev_x + dev_l
    for dev in everyone:
        pl.semaphore_signal(barrier, inc=1, device_id=dev, device_id_type=MESH)

    def remote(src, dst, s, r, dev):
        return pltpu.make_async_remote_copy(
            src_ref=src, dst_ref=dst, send_sem=s, recv_sem=r, device_id=dev, device_id_type=MESH
        )

    def root_l(t):
        return (1 - t // 4) * 3 * (t // 2) + t // 4 * (1 + t % 2)

    def root_c(t):
        return t % 2 + t // 6 * (1 - 2 * (t % 2))

    def columns(hh, pp):
        return pl.ds(pl.multiple_of((hh * 2 + pp) * DP, DP), DP)

    half = pl.ds(pl.multiple_of(c * DB, DB), DB)

    def half_columns(hh, pp):
        return pl.ds(pl.multiple_of((hh * 2 + pp) * DP + c * DB, DB), DB)

    def x_own(t):
        return pltpu.make_async_copy(
            x_hbm.at[root_l(t), :, root_c(t), :, columns(h, pair)], xs.at[t, OWN], sem_own
        )

    def x_push(t, cols, block, s, dev):
        return remote(
            x_hbm.at[root_l(t), x, root_c(t), :, cols], xs.at[t, block, x, :, half], s, xp_r.at[t], dev
        )

    def x_b(t):
        return x_push(t, half_columns(h, 1 - pair), BESIDE, xb_s, dev_b)

    def x_z(t):
        return x_push(t, half_columns(h2, pair), ACROSS, xz_s, dev_z)

    def x_d(t):
        return x_push(t, half_columns(h2, 1 - pair), DIAGONAL, xd_s, dev_d)

    def x_x(t, d):
        part = xs.at[t, 1:4, x, :, half]
        return remote(part, part, xx_s.at[d], xx_r.at[t], dev_x[d])

    def x_c(t):
        part = xs.at[t, 1:4, :, :, half]
        return remote(part, part, xc_s, xc_r.at[t], dev_c)

    w_rows = pl.ds(pl.multiple_of(side * DB, DB), DB)

    def f_cols(f):
        return pl.ds(pl.multiple_of(f * FC, FC), FC)

    def w_a(f):
        part = ws.at[f, w_rows]
        return remote(part, part, w_s, w_r.at[f], dev_a)

    def hid_b(k):
        return remote(send_b.at[k], recv_b.at[k], b_s, b_r.at[k], dev_b)

    def hid_z(k):
        return remote(send_z.at[k], recv_z.at[k], z_s, z_r.at[k], dev_z)

    def grad_z(k):
        return remote(hg.at[k, OWN], hg.at[k, ACROSS], gz_s, gz_r.at[k], dev_z)

    def grad_0(k):
        return remote(hg.at[k, OWN], hg.at[k, BESIDE], g0_s, g_r.at[k], dev_b)

    def grad_1(k):
        return remote(hg.at[k, ACROSS], hg.at[k, DIAGONAL], g1_s, g_r.at[k], dev_b)

    def term_a(f):
        return remote(send_a.at[f], recv_a.at[f], a_s, a_r.at[f], dev_a)

    def gw_out(f):
        return pltpu.make_async_copy(gout.at[f], gw_hbm.at[:, f_cols(f)], sem_gw)

    def red_c(n):
        return remote(send_c.at[n], recv_c.at[n], c_s, c_r.at[n], dev_c)

    def red_x(n, d):
        return remote(send_x.at[n, d], recv_x.at[n, d], rx_s.at[d], rx_r.at[n], dev_x[d])

    def red_up(n):
        return remote(send_l.at[n], recv_l.at[n, 0], l_s, l_r.at[n, 0], at(h, y, (l + 1) % 4, x, c))

    def red_down(n):
        return remote(send_l.at[n], recv_l.at[n, 1], l_s, l_r.at[n, 1], at(h, y, (l + 3) % 4, x, c))

    def red_far(n):
        return remote(send_l.at[n], recv_f, l_s, lf_r, at(h, y, (l + 2) % 4, x, c))

    def red_send(t):
        far = (t // 2 == H - 1) & (((l == 3) & (root_l(t) == 1)) | ((l == 0) & (root_l(t) == 2)))

        @pl.when((l > root_l(t)) & jnp.logical_not(far))
        def _():
            red_down(t // 2).start()

        @pl.when((l < root_l(t)) & jnp.logical_not(far))
        def _():
            red_up(t // 2).start()

        @pl.when(far)
        def _():
            red_far(t // 2).start()

    mine = h * 2 + pair

    def final(n):
        return remote(send_f.at[n], fin.at[mine], f_s, f_r, (dev_z, dev_d, dev_b)[n])

    def ig_out(n):
        return pltpu.make_async_copy(fin.at[n], ig_hbm.at[:, n * DP : (n + 1) * DP], sem_ig)

    codes_copy = pltpu.make_async_copy(codes_hbm, codes, sem_in.at[0])
    scales_copy = pltpu.make_async_copy(scales_hbm, scales, sem_in.at[1])
    act_copy = pltpu.make_async_copy(act_hbm, act, sem_in.at[2])
    scales_copy.start()
    codes_copy.start()
    for t in range(T):
        x_own(t).start()
    act_copy.start()
    pl.semaphore_wait(barrier, len(everyone))

    def x_start(t):
        x_d(t).start()
        x_z(t).start()
        x_b(t).start()

    def x_share(t):
        part = xs.at[t, 1:4, x, :, half]
        remote(part, part, xc_s, xp_r.at[t], dev_c).wait_recv()
        for d in range(3):
            x_x(t, d).start()

    def x_core(t):
        part = xs.at[t, 1:4, 0:3, :, half]
        remote(part, part, xc_s, xx_r.at[t], dev_c).wait_recv()
        x_c(t).start()

    x_start(0)
    x_start(1)
    scales_copy.wait()
    codes_copy.wait()
    scale = jnp.broadcast_to(scales[...].astype(F32).reshape(1, DB), (128, DB)).T
    for f in range(F):
        for j in range(FC // 128):
            value = codes[:, f * FC + j * 128 : f * FC + (j + 1) * 128].astype(F32) * scale
            ws[f, w_rows, j * 128 : (j + 1) * 128] = value.astype(BF16)
    w_a(0).start()
    w_a(1).start()
    x_start(2)
    w_a(2).start()
    for t in range(3, T):
        x_start(t)
    term[...] = jnp.zeros_like(term)
    x_share(0)
    act_copy.wait()
    pltpu.make_async_copy(xs.at[:, OWN], xs.at[:, OWN], sem_own).wait()
    x_share(1)
    x_core(0)
    x_share(2)
    x_core(1)

    def stage(step, offset, body):
        @pl.when((step >= offset) & (step < offset + K))
        def _():
            t, f = chunk(step - offset)
            body(t, f, t * F + f)

    def stage_t(step, offset, body):
        @pl.when((step >= offset) & (step < offset + K))
        def _():
            t, f = chunk(step - offset)

            @pl.when(f == F - 1)
            def _():
                body(t)

    def average(f):
        term_a(f).wait_recv()
        total = term[f, :, w_rows] + recv_a[f].astype(F32)
        gout[f] = total.T
        gw_out(f).start()

    def end(t):
        return ((l == 0) & (root_l(t) > 0)) | ((l == 3) & (root_l(t) < 3)) | ((l != root_l(t)) & (t // 2 == H - 1))

    def step_body(step, carry):
        def s4(t, f, k):
            hid_b(k).wait_recv()
            send_z[k] = (keep[k, 1] + recv_b[k, 0].astype(F32)).astype(BF16)
            hid_z(k).start()
            keep[k, 0] += recv_b[k, 1].astype(F32)

        stage(step, O_S4, s4)

        def s5(t, f, k):
            hid_z(k).wait_recv()
            hidden = keep[k, 0] + recv_z[k].astype(F32)
            given = act[root_l(t), :, root_c(t), :, f_cols(f)].reshape(TC, FC)
            hg[k, OWN] = (given.astype(F32) * gelu_slope(hidden)).astype(BF16)
            grad_z(k).start()
            grad_0(k).start()

        stage(step, O_S5, s5)

        def s6(t, f, k):
            grad_z(k).wait_recv()
            grad_1(k).start()

        stage(step, O_S6, s6)

        def s3(t, f, k):

            @pl.when(f == 0)
            def _():
                x_c(t).wait_recv()

            @pl.when(t == 0)
            def _():
                w_a(f).wait_recv()

            both = jnp.dot(xs[t].reshape(4 * TC, DP), ws[f], preferred_element_type=F32)
            send_b[k] = both[2 * TC :].astype(BF16).reshape(2, TC, FC)
            hid_b(k).start()
            keep[k] = both[: 2 * TC].reshape(2, TC, FC)

        stage(step, 0, s3)

        @pl.when(step == 0)
        def _():
            x_share(3)

        @pl.when(step < 2)
        def _():
            x_core(step + 2)

        @pl.when((step % 2 == 0) & (step >= 4) & (step <= 10))
        def _():
            x_share((step + 4) // 2)

        @pl.when((step % 2 == 0) & (step >= 6) & (step <= 12))
        def _():
            x_core((step + 2) // 2)

        def r1(t):
            n = t // 2

            @pl.when(c == root_c(t))
            def _():
                red_c(n).wait_recv()
                for d in (1, 2, 3, 0):
                    xx = (x + d) % 4
                    for block in range(4):
                        rows = pl.ds(pl.multiple_of(block * TC + xx * 16, 16), 16)
                        value = acc[n, rows, :] + recv_c[n, rows, :].astype(F32)
                        if d == 0:
                            keep_x[n, block] = value
                        else:
                            send_x[n, d - 1, block] = value.astype(BF16)
                    if d:
                        red_x(n, d - 1).start()

        stage_t(step, O_R1, r1)

        def s7(t, f, k):
            beside = hg.at[k, 2:4]
            remote(beside, beside, g0_s, g_r.at[k], dev_b).wait_recv()
            grads = hg[k].reshape(4 * TC, FC)

            def partial(cols):
                return sum(
                    lax.dot_general(
                        hg[t * F + n].reshape(4 * TC, FC), ws[n, cols, :],
                        (((1,), (1,)), ((), ())), preferred_element_type=F32,
                    )
                    for n in range(F)
                )

            @pl.when((f == F - 1) & (c == root_c(t)))
            def _():
                for j in range(DP // COLS):
                    cols = pl.ds(j * COLS, COLS)
                    acc[t // 2, :, cols] = partial(cols)

            @pl.when((f == F - 1) & (c != root_c(t)))
            def _():
                for j in range(DP // COLS):
                    cols = pl.ds(j * COLS, COLS)
                    send_c[t // 2, :, cols] = partial(cols).astype(BF16)
                red_c(t // 2).start()

            for j in range(DP // COLS):
                cols = pl.ds(j * COLS, COLS)
                term[f, :, cols] += lax.dot_general(
                    grads, xs[t, :, :, :, cols].reshape(4 * TC, COLS),
                    (((0,), (0,)), ((), ())), preferred_element_type=F32,
                )

            @pl.when(t == T - 1)
            def _():
                other = pl.ds(pl.multiple_of((1 - side) * DB, DB), DB)
                send_a[f] = term[f, :, other].astype(BF16)
                term_a(f).start()

        stage(step, O_S7, s7)

        def r2(t):
            n = t // 2

            @pl.when(c == root_c(t))
            def _():
                remote(send_x.at[n], recv_x.at[n], rx_s.at[0], rx_r.at[n], dev_c).wait_recv()
                value = keep_x[n]
                for d in range(3):
                    value = value + recv_x[n, d].astype(F32)

                keep_x[n] = value

                @pl.when(end(t))
                def _():
                    send_l[n] = value.astype(BF16)
                    red_send(t)

        stage_t(step, O_R2, r2)

        for depth in (1, 2):

            def r3(t):
                n = t // 2

                @pl.when((c == root_c(t)) & (l < root_l(t)) & (l == depth) & (n < H - 1))
                def _():
                    red_up(n).wait_recv()
                    send_l[n] = (keep_x[n] + recv_l[n, 0].astype(F32)).astype(BF16)
                    red_up(n).start()

                @pl.when((c == root_c(t)) & (l > root_l(t)) & (3 - l == depth) & (n < H - 1))
                def _():
                    red_down(n).wait_recv()
                    send_l[n] = (keep_x[n] + recv_l[n, 1].astype(F32)).astype(BF16)
                    red_down(n).start()

            stage_t(step, O_R2 + O_R3 * depth, r3)

        return carry

    lax.fori_loop(0, STEPS, step_body, 0)

    for f in range(F - 1):
        average(f)

    last = l // 3 + (l + 1) // 2 % 2 * (2 + (l + c + 1) % 2)

    @pl.when(l > 0)
    def _():
        red_up(last).wait_recv()
        keep_x[last] += recv_l[last, 0].astype(F32)

    @pl.when(l < 3)
    def _():
        red_down(last).wait_recv()
        keep_x[last] += recv_l[last, 1].astype(F32)

    @pl.when(last == H - 1)
    def _():
        red_far(last).wait_recv()
        keep_x[last] += recv_f[...].astype(F32)

    value = keep_x[last]
    value = value.astype(BF16)
    fin[mine] = value[OWN]
    for n in range(3):
        send_f[n] = value[n + 1]
        final(n).start()

    average(F - 1)

    def left(buffer, s):
        remote(buffer, buffer, s, f_r, dev_c).wait_send()

    pushed = xs.at[:, BESIDE, x, :, half]
    for s in (xb_s, xz_s, xd_s):
        left(pushed, s)
    for d in range(3):
        left(xs.at[:, 1:4, x, :, half], xx_s.at[d])
        left(send_x.at[:, d], rx_s.at[d])
    left(xs.at[:, 1:4, :, :, half], xc_s)
    left(ws.at[:, w_rows], w_s)
    left(send_b, b_s)
    left(send_z, z_s)
    left(hg.at[:, OWN], gz_s)
    left(hg.at[:, OWN], g0_s)
    left(hg.at[:, ACROSS], g1_s)
    left(send_a, a_s)
    left(send_c, c_s)
    left(send_l.at[0:3], l_s)
    left(send_f, f_s)

    remote(fin.at[0:3], fin.at[0:3], f_s, f_r, dev_c).wait_recv()
    for n in range(4):
        ig_out(n).start()
    pltpu.make_async_copy(gout, gout, sem_gw).wait()
    pltpu.make_async_copy(fin, fin, sem_ig).wait()


def scratch():
    dma = pltpu.SemaphoreType.DMA
    return [
        pltpu.VMEM((T, 4, 4, 16, DP), BF16),
        pltpu.VMEM((F, DP, FC), BF16),
        pltpu.VMEM((DB, 768), BF16),
        pltpu.VMEM((DB,), BF16),
        pltpu.VMEM((4, 4, 2, 16, 768), BF16),
        pltpu.VMEM((K, 2, TC, FC), BF16),
        pltpu.VMEM((K, 2, TC, FC), BF16),
        pltpu.VMEM((K, 2, TC, FC), F32),
        pltpu.VMEM((K, TC, FC), BF16),
        pltpu.VMEM((K, TC, FC), BF16),
        pltpu.VMEM((K, 4, TC, FC), BF16),
        pltpu.VMEM((F, FC, DP), F32),
        pltpu.VMEM((H, 4 * TC, DP), F32),
        pltpu.VMEM((H, 4 * TC, DP), BF16),
        pltpu.VMEM((H, 4 * TC, DP), BF16),
        pltpu.VMEM((H, 3, 4, 16, DP), BF16),
        pltpu.VMEM((H, 3, 4, 16, DP), BF16),
        pltpu.VMEM((H, 4, 16, DP), F32),
        pltpu.VMEM((H, 4, 16, DP), BF16),
        pltpu.VMEM((H, 2, 4, 16, DP), BF16),
        pltpu.VMEM((4, 16, DP), BF16),
        pltpu.VMEM((3, 16, DP), BF16),
        pltpu.VMEM((4, 16, DP), BF16),
        pltpu.VMEM((F, FC, DB), BF16),
        pltpu.VMEM((F, FC, DB), BF16),
        pltpu.VMEM((F, DB, FC), F32),
        dma, dma((3,)), dma, dma,
        dma, dma, dma, dma((T,)), dma((3,)), dma((T,)), dma, dma((T,)),
        dma, dma((F,)), dma, dma((K,)), dma, dma((K,)), dma, dma((K,)), dma, dma, dma((K,)),
        dma, dma((F,)), dma, dma((H,)), dma((3,)), dma((H,)), dma, dma((H, 2)), dma, dma, dma,
    ]


def local(inputs, act_grad, in_codes, in_scales):
    input_grad, in_grad = pl.pallas_call(
        kernel,
        out_shape=(
            jax.ShapeDtypeStruct((16, 6144), BF16),
            jax.ShapeDtypeStruct((768, 768), F32),
        ),
        in_specs=[pl.BlockSpec(memory_space=pl.ANY)] * 4,
        out_specs=(
            pl.BlockSpec(memory_space=pl.ANY),
            pl.BlockSpec(memory_space=pl.ANY),
        ),
        scratch_shapes=scratch(),
        compiler_params=pltpu.CompilerParams(
            collective_id=0, has_side_effects=True, vmem_limit_bytes=60 * 1024 * 1024
        ),
        cost_estimate=pl.CostEstimate(
            flops=3 * 2 * 512 * 6144 * 768, bytes_accessed=12 * 1024 * 1024, transcendentals=512 * 768
        ),
        name="ffn_in_backward",
    )(
        inputs.reshape(4, 4, 2, 16, 6144),
        act_grad.reshape(4, 4, 2, 16, 768),
        in_codes,
        in_scales,
    )
    return input_grad, in_grad * 0.125


def solution(mesh):
    return jax.shard_map(
        local,
        mesh=mesh,
        in_specs=(P("outer", None), P("outer", "inner"), P("outer", "inner"), P("outer")),
        out_specs=(P(("outer", "inner"), None), P("outer", "inner")),
        check_vma=False,
    )
```

```python
import functools

import jax
import jax.numpy as jnp
from jax import lax
from jax.experimental import pallas as pl
from jax.experimental.pallas import tpu as pltpu
from jax.sharding import PartitionSpec as P

coef = 0.7978845608
cubic = 0.044715

MESH = pl.DeviceIdType.MESH
F32 = jnp.float32
BF16 = jnp.bfloat16

F = 3
H = 4
T = 2 * H
K = T * F
FC = 256
TC = 64
DB = 768
DP = 1536
COLS = 256
HALVES = (slice(0, DB), slice(DB, DP))
OWN, ACROSS, DIAGONAL, BESIDE = 0, 1, 2, 3

O_S4, O_S5, O_S6, O_S7, O_R1, O_R2 = 3, 6, 9, 12, 13, 24
STEPS = K + O_R2


def chunk(n):
    late = n // 12
    r = n % 12
    e = r // 6
    q = r % 6
    s = q // 2
    t = 4 + (1 - e) * (s // 2 * 2 + (1 - s % 2) * (q % 2)) + e * (1 + s)
    f = (1 - e) * (s % 2) * (1 + q % 2) + e * (1 + q % 2)
    return (1 - late) * (r % 4) + late * t, (1 - late) * (r // 4) + late * f


def gelu_slope(value):
    tangent = jnp.tanh(coef * (value + cubic * value * value * value))
    return 0.5 * (1.0 + tangent) + 0.5 * value * (1.0 - tangent * tangent) * coef * (
        1.0 + 3.0 * cubic * value * value
    )


def kernel(
    x_hbm, act_hbm, codes_hbm, scales_hbm, ig_hbm, gw_hbm,
    xs, ws, codes, scales, act, send_b, recv_b, keep, send_z, recv_z, hg, term,
    acc, send_c, recv_c, send_x, recv_x, keep_x, send_l, recv_l,
    send_f, fin, send_a, recv_a, gout,
    sem_own, sem_in, sem_gw, sem_ig,
    xb_s, xz_s, xd_s, xp_r, xx_s, xx_r, xc_s, xc_r,
    w_s, w_r, b_s, b_r, z_s, z_r, gz_s, gz_r, g0_s, g1_s, g_r,
    a_s, a_r, c_s, c_r, rx_s, rx_r, l_s, l_r, f_s, f_r,
):
    o = lax.axis_index("outer")
    i = lax.axis_index("inner")
    h, y = o // 4, o % 4
    l, x, c = i // 8, (i // 2) % 4, i % 2
    pair, side = y // 2, y % 2
    h2, yb = 1 - h, 3 - y
    ya = pair * 2 + (1 - side)

    def at(hh, yy, ll, xx, cc):
        return (hh * 4 + yy, (ll * 4 + xx) * 2 + cc)

    dev_a = at(h, ya, l, x, c)
    dev_b = at(h, yb, l, x, c)
    dev_z = at(h2, y, l, x, c)
    dev_d = at(h2, yb, l, x, c)
    dev_c = at(h, y, l, x, 1 - c)
    dev_x = [at(h, y, l, (x + d) % 4, c) for d in (1, 2, 3)]
    dev_l = [at(h, y, (l + d) % 4, x, c) for d in (1, 2, 3)]

    barrier = pltpu.get_barrier_semaphore()
    everyone = [dev_a, dev_b, dev_z, dev_d, dev_c] + dev_x + dev_l
    for dev in everyone:
        pl.semaphore_signal(barrier, inc=1, device_id=dev, device_id_type=MESH)

    def remote(src, dst, s, r, dev):
        return pltpu.make_async_remote_copy(
            src_ref=src, dst_ref=dst, send_sem=s, recv_sem=r, device_id=dev, device_id_type=MESH
        )

    def root_l(t):
        return (1 - t // 4) * 3 * (t // 2) + t // 4 * (1 + t % 2)

    def root_c(t):
        return t % 2 + t // 6 * (1 - 2 * (t % 2))

    def columns(hh, pp):
        return pl.ds(pl.multiple_of((hh * 2 + pp) * DP, DP), DP)

    half = pl.ds(pl.multiple_of(c * DB, DB), DB)

    def half_columns(hh, pp):
        return pl.ds(pl.multiple_of((hh * 2 + pp) * DP + c * DB, DB), DB)

    def x_own(t):
        return pltpu.make_async_copy(
            x_hbm.at[root_l(t), :, root_c(t), :, columns(h, pair)], xs.at[t, OWN], sem_own
        )

    def x_push(t, cols, block, s, dev):
        return remote(
            x_hbm.at[root_l(t), x, root_c(t), :, cols], xs.at[t, block, x, :, half], s, xp_r.at[t], dev
        )

    def x_b(t):
        return x_push(t, half_columns(h, 1 - pair), BESIDE, xb_s, dev_b)

    def x_z(t):
        return x_push(t, half_columns(h2, pair), ACROSS, xz_s, dev_z)

    def x_d(t):
        return x_push(t, half_columns(h2, 1 - pair), DIAGONAL, xd_s, dev_d)

    def x_x(t, d):
        part = xs.at[t, 1:4, x, :, half]
        return remote(part, part, xx_s.at[d], xx_r.at[t], dev_x[d])

    def x_c(t):
        part = xs.at[t, 1:4, :, :, half]
        return remote(part, part, xc_s, xc_r.at[t], dev_c)

    w_rows = pl.ds(pl.multiple_of(side * DB, DB), DB)

    def f_cols(f):
        return pl.ds(pl.multiple_of(f * FC, FC), FC)

    def w_a(f):
        part = ws.at[f, w_rows]
        return remote(part, part, w_s, w_r.at[f], dev_a)

    def hid_b(k):
        return remote(send_b.at[k], recv_b.at[k], b_s, b_r.at[k], dev_b)

    def hid_z(k):
        return remote(send_z.at[k], recv_z.at[k], z_s, z_r.at[k], dev_z)

    def grad_z(k):
        return remote(hg.at[k, OWN], hg.at[k, ACROSS], gz_s, gz_r.at[k], dev_z)

    def grad_0(k):
        return remote(hg.at[k, OWN], hg.at[k, BESIDE], g0_s, g_r.at[k], dev_b)

    def grad_1(k):
        return remote(hg.at[k, ACROSS], hg.at[k, DIAGONAL], g1_s, g_r.at[k], dev_b)

    def term_a(f):
        return remote(send_a.at[f], recv_a.at[f], a_s, a_r.at[f], dev_a)

    def gw_out(f):
        return pltpu.make_async_copy(gout.at[f], gw_hbm.at[:, f_cols(f)], sem_gw)

    def red_c(n, s):
        return remote(send_c.at[n, :, HALVES[s]], recv_c.at[n, :, HALVES[s]], c_s, c_r.at[n, s], dev_c)

    def red_x(n, d, s):
        part = (n, d, slice(None), slice(None), HALVES[s])
        return remote(send_x.at[part], recv_x.at[part], rx_s.at[d], rx_r.at[n, s], dev_x[d])

    def red_l(n, s, away):
        part = send_l.at[n, :, :, HALVES[s]]
        return remote(
            part, recv_l.at[away - 1, :, :, HALVES[s]], l_s, l_r.at[away - 1, s], at(h, y, (l + 4 - away) % 4, x, c)
        )

    mine = h * 2 + pair

    def final(n, s):
        part = send_f.at[n, :, HALVES[s]]
        return remote(part, fin.at[mine, :, HALVES[s]], f_s, f_r, (dev_z, dev_d, dev_b)[n])

    def ig_out(n):
        return pltpu.make_async_copy(fin.at[n], ig_hbm.at[:, n * DP : (n + 1) * DP], sem_ig)

    codes_copy = pltpu.make_async_copy(codes_hbm, codes, sem_in.at[0])
    scales_copy = pltpu.make_async_copy(scales_hbm, scales, sem_in.at[1])
    act_copy = pltpu.make_async_copy(act_hbm, act, sem_in.at[2])
    scales_copy.start()
    codes_copy.start()
    for t in range(T):
        x_own(t).start()
    act_copy.start()
    pl.semaphore_wait(barrier, len(everyone))

    def x_start(t):
        x_d(t).start()
        x_z(t).start()
        x_b(t).start()

    def x_share(t):
        part = xs.at[t, 1:4, x, :, half]
        remote(part, part, xc_s, xp_r.at[t], dev_c).wait_recv()
        for d in range(3):
            x_x(t, d).start()

    def x_core(t):
        part = xs.at[t, 1:4, 0:3, :, half]
        remote(part, part, xc_s, xx_r.at[t], dev_c).wait_recv()
        x_c(t).start()

    x_start(0)
    x_start(1)
    scales_copy.wait()
    codes_copy.wait()
    scale = jnp.broadcast_to(scales[...].astype(F32).reshape(1, DB), (128, DB)).T
    for f in range(F):
        for j in range(FC // 128):
            value = codes[:, f * FC + j * 128 : f * FC + (j + 1) * 128].astype(F32) * scale
            ws[f, w_rows, j * 128 : (j + 1) * 128] = value.astype(BF16)
    w_a(0).start()
    w_a(1).start()
    x_start(2)
    w_a(2).start()
    for t in range(3, T):
        x_start(t)
    term[...] = jnp.zeros_like(term)
    x_share(0)
    act_copy.wait()
    pltpu.make_async_copy(xs.at[:, OWN], xs.at[:, OWN], sem_own).wait()
    x_share(1)
    x_core(0)
    x_share(2)
    x_core(1)

    def stage(step, offset, body):
        @pl.when((step >= offset) & (step < offset + K))
        def _():
            t, f = chunk(step - offset)
            body(t, f, t * F + f)

    def stage_t(step, offset, body):
        @pl.when((step >= offset) & (step < offset + K))
        def _():
            t, f = chunk(step - offset)

            @pl.when(f == F - 1)
            def _():
                body(t)

    def average(f):
        term_a(f).wait_recv()
        total = term[f, :, w_rows] + recv_a[f].astype(F32)
        gout[f] = total.T
        gw_out(f).start()

    def step_body(step, carry):
        def s4(t, f, k):
            hid_b(k).wait_recv()
            send_z[k] = (keep[k, 1] + recv_b[k, 0].astype(F32)).astype(BF16)
            hid_z(k).start()
            keep[k, 0] += recv_b[k, 1].astype(F32)

        stage(step, O_S4, s4)

        def s5(t, f, k):
            hid_z(k).wait_recv()
            hidden = keep[k, 0] + recv_z[k].astype(F32)
            given = act[root_l(t), :, root_c(t), :, f_cols(f)].reshape(TC, FC)
            hg[k, OWN] = (given.astype(F32) * gelu_slope(hidden)).astype(BF16)
            grad_z(k).start()
            grad_0(k).start()

        stage(step, O_S5, s5)

        def s6(t, f, k):
            grad_z(k).wait_recv()
            grad_1(k).start()

        stage(step, O_S6, s6)

        def s3(t, f, k):

            @pl.when(f == 0)
            def _():
                x_c(t).wait_recv()

            @pl.when(t == 0)
            def _():
                w_a(f).wait_recv()

            both = jnp.dot(xs[t].reshape(4 * TC, DP), ws[f], preferred_element_type=F32)
            send_b[k] = both[2 * TC :].astype(BF16).reshape(2, TC, FC)
            hid_b(k).start()
            keep[k] = both[: 2 * TC].reshape(2, TC, FC)

        stage(step, 0, s3)

        @pl.when(step == 0)
        def _():
            x_share(3)

        @pl.when(step < 2)
        def _():
            x_core(step + 2)

        @pl.when((step % 2 == 0) & (step >= 4) & (step <= 10))
        def _():
            x_share((step + 4) // 2)

        @pl.when((step % 2 == 0) & (step >= 6) & (step <= 12))
        def _():
            x_core((step + 2) // 2)

        def r1(t):
            n = t // 2

            @pl.when(c == root_c(t))
            def _():
                for s in range(2):
                    cols = HALVES[s]
                    red_c(n, s).wait_recv()
                    for d in (1, 2, 3, 0):
                        xx = (x + d) % 4
                        for block in range(4):
                            rows = pl.ds(pl.multiple_of(block * TC + xx * 16, 16), 16)
                            value = acc[n, rows, cols] + recv_c[n, rows, cols].astype(F32)
                            if d == 0:
                                keep_x[n, block, :, cols] = value
                            else:
                                send_x[n, d - 1, block, :, cols] = value.astype(BF16)
                        if d:
                            red_x(n, d - 1, s).start()

        stage_t(step, O_R1, r1)

        def s7(t, f, k):
            beside = hg.at[k, 2:4]
            remote(beside, beside, g0_s, g_r.at[k], dev_b).wait_recv()
            grads = hg[k].reshape(4 * TC, FC)

            def partial(cols):
                return sum(
                    lax.dot_general(
                        hg[t * F + n].reshape(4 * TC, FC), ws[n, cols, :],
                        (((1,), (1,)), ((), ())), preferred_element_type=F32,
                    )
                    for n in range(F)
                )

            @pl.when((f == F - 1) & (c == root_c(t)))
            def _():
                for j in range(DP // COLS):
                    cols = pl.ds(j * COLS, COLS)
                    acc[t // 2, :, cols] = partial(cols)

            @pl.when((f == F - 1) & (c != root_c(t)))
            def _():
                for s in range(2):
                    for j in range(DB // COLS):
                        cols = pl.ds(s * DB + j * COLS, COLS)
                        send_c[t // 2, :, cols] = partial(cols).astype(BF16)
                    red_c(t // 2, s).start()

            for j in range(DP // COLS):
                cols = pl.ds(j * COLS, COLS)
                term[f, :, cols] += lax.dot_general(
                    grads, xs[t, :, :, :, cols].reshape(4 * TC, COLS),
                    (((0,), (0,)), ((), ())), preferred_element_type=F32,
                )

            @pl.when(t == T - 1)
            def _():
                other = pl.ds(pl.multiple_of((1 - side) * DB, DB), DB)
                send_a[f] = term[f, :, other].astype(BF16)
                term_a(f).start()

        stage(step, O_S7, s7)

        def r2(t):
            n = t // 2

            @pl.when(c == root_c(t))
            def _():
                for s in range(2):
                    cols = HALVES[s]
                    part = recv_x.at[n, :, :, :, cols]
                    remote(part, part, rx_s.at[0], rx_r.at[n, s], dev_c).wait_recv()
                    value = keep_x[n, :, :, cols]
                    for d in range(3):
                        value = value + recv_x[n, d, :, :, cols].astype(F32)
                    keep_x[n, :, :, cols] = value
                    send_l[n, :, :, cols] = value.astype(BF16)

                    for away in (1, 2, 3):

                        @pl.when((l - root_l(t) + 4) % 4 == away)
                        def _(s=s, away=away):
                            red_l(n, s, away).start()

        stage_t(step, O_R2, r2)

        return carry

    lax.fori_loop(0, STEPS, step_body, 0)

    for f in range(F - 1):
        average(f)

    last = l // 3 + (l + 1) // 2 % 2 * (2 + (l + c + 1) % 2)

    for s in range(2):
        cols = HALVES[s]

        value = keep_x[last, :, :, cols]
        for away in (1, 2, 3):
            red_l(0, s, away).wait_recv()
            value = value + recv_l[away - 1, :, :, cols].astype(F32)
        value = value.astype(BF16)
        fin[mine, :, cols] = value[OWN]
        for n in range(3):
            send_f[n, :, cols] = value[n + 1]
            final(n, s).start()

    average(F - 1)

    def left(buffer, s):
        remote(buffer, buffer, s, f_r, dev_c).wait_send()

    pushed = xs.at[:, BESIDE, x, :, half]
    for s in (xb_s, xz_s, xd_s):
        left(pushed, s)
    for d in range(3):
        left(xs.at[:, 1:4, x, :, half], xx_s.at[d])
        left(send_x.at[:, d], rx_s.at[d])
    left(xs.at[:, 1:4, :, :, half], xc_s)
    left(ws.at[:, w_rows], w_s)
    left(send_b, b_s)
    left(send_z, z_s)
    left(hg.at[:, OWN], gz_s)
    left(hg.at[:, OWN], g0_s)
    left(hg.at[:, ACROSS], g1_s)
    left(send_a, a_s)
    left(send_c, c_s)
    left(send_l.at[0:3], l_s)
    left(send_f, f_s)

    remote(fin.at[0:3], fin.at[0:3], f_s, f_r, dev_c).wait_recv()
    for n in range(4):
        ig_out(n).start()
    pltpu.make_async_copy(gout, gout, sem_gw).wait()
    pltpu.make_async_copy(fin, fin, sem_ig).wait()


def scratch():
    dma = pltpu.SemaphoreType.DMA
    return [
        pltpu.VMEM((T, 4, 4, 16, DP), BF16),
        pltpu.VMEM((F, DP, FC), BF16),
        pltpu.VMEM((DB, 768), BF16),
        pltpu.VMEM((DB,), BF16),
        pltpu.VMEM((4, 4, 2, 16, 768), BF16),
        pltpu.VMEM((K, 2, TC, FC), BF16),
        pltpu.VMEM((K, 2, TC, FC), BF16),
        pltpu.VMEM((K, 2, TC, FC), F32),
        pltpu.VMEM((K, TC, FC), BF16),
        pltpu.VMEM((K, TC, FC), BF16),
        pltpu.VMEM((K, 4, TC, FC), BF16),
        pltpu.VMEM((F, FC, DP), F32),
        pltpu.VMEM((H, 4 * TC, DP), F32),
        pltpu.VMEM((H, 4 * TC, DP), BF16),
        pltpu.VMEM((H, 4 * TC, DP), BF16),
        pltpu.VMEM((H, 3, 4, 16, DP), BF16),
        pltpu.VMEM((H, 3, 4, 16, DP), BF16),
        pltpu.VMEM((H, 4, 16, DP), F32),
        pltpu.VMEM((H, 4, 16, DP), BF16),
        pltpu.VMEM((3, 4, 16, DP), BF16),
        pltpu.VMEM((3, 16, DP), BF16),
        pltpu.VMEM((4, 16, DP), BF16),
        pltpu.VMEM((F, FC, DB), BF16),
        pltpu.VMEM((F, FC, DB), BF16),
        pltpu.VMEM((F, DB, FC), F32),
        dma, dma((3,)), dma, dma,
        dma, dma, dma, dma((T,)), dma((3,)), dma((T,)), dma, dma((T,)),
        dma, dma((F,)), dma, dma((K,)), dma, dma((K,)), dma, dma((K,)), dma, dma, dma((K,)),
        dma, dma((F,)), dma, dma((H, 2)), dma((3,)), dma((H, 2)), dma, dma((3, 2)), dma, dma,
    ]


def local(inputs, act_grad, in_codes, in_scales):
    input_grad, in_grad = pl.pallas_call(
        kernel,
        out_shape=(
            jax.ShapeDtypeStruct((16, 6144), BF16),
            jax.ShapeDtypeStruct((768, 768), F32),
        ),
        in_specs=[pl.BlockSpec(memory_space=pl.ANY)] * 4,
        out_specs=(
            pl.BlockSpec(memory_space=pl.ANY),
            pl.BlockSpec(memory_space=pl.ANY),
        ),
        scratch_shapes=scratch(),
        compiler_params=pltpu.CompilerParams(
            collective_id=0, has_side_effects=True, vmem_limit_bytes=60 * 1024 * 1024
        ),
        cost_estimate=pl.CostEstimate(
            flops=3 * 2 * 512 * 6144 * 768, bytes_accessed=12 * 1024 * 1024, transcendentals=512 * 768
        ),
        name="ffn_in_backward",
    )(
        inputs.reshape(4, 4, 2, 16, 6144),
        act_grad.reshape(4, 4, 2, 16, 768),
        in_codes,
        in_scales,
    )
    return input_grad, in_grad * 0.125


def solution(mesh):
    return jax.shard_map(
        local,
        mesh=mesh,
        in_specs=(P("outer", None), P("outer", "inner"), P("outer", "inner"), P("outer")),
        out_specs=(P(("outer", "inner"), None), P("outer", "inner")),
        check_vma=False,
    )
```

```python
import functools

import jax
import jax.numpy as jnp
from jax import lax
from jax.experimental import pallas as pl
from jax.experimental.pallas import tpu as pltpu
from jax.sharding import PartitionSpec as P

coef = 0.7978845608
cubic = 0.044715

MESH = pl.DeviceIdType.MESH
F32 = jnp.float32
BF16 = jnp.bfloat16

F = 3
H = 4
T = 2 * H
K = T * F
FC = 256
TC = 64
DB = 768
DP = 1536
COLS = 256
HALVES = (slice(0, DB), slice(DB, DP))
OWN, ACROSS, DIAGONAL, BESIDE = 0, 1, 2, 3

O_S4, O_S5, O_S6, O_S7, O_R1, O_R2 = 3, 6, 9, 12, 13, 24
STEPS = K + O_R2


def chunk(n):
    late = n // 12
    r = n % 12
    e = r // 6
    q = r % 6
    s = q // 2
    t = 4 + (1 - e) * (s // 2 * 2 + (1 - s % 2) * (q % 2)) + e * (1 + s)
    f = (1 - e) * (s % 2) * (1 + q % 2) + e * (1 + q % 2)
    return (1 - late) * (r % 4) + late * t, (1 - late) * (r // 4) + late * f


def gelu_slope(value):
    tangent = jnp.tanh(coef * (value + cubic * value * value * value))
    return 0.5 * (1.0 + tangent) + 0.5 * value * (1.0 - tangent * tangent) * coef * (
        1.0 + 3.0 * cubic * value * value
    )


def kernel(
    x_hbm, act_hbm, codes_hbm, scales_hbm, ig_hbm, gw_hbm,
    xs, ws, codes, scales, act, send_b, recv_b, keep, send_z, recv_z, hg, term,
    acc, send_c, recv_c, send_x, recv_x, keep_x, send_l, recv_l,
    send_f, fin, send_a, recv_a, gout,
    sem_own, sem_in, sem_gw, sem_ig,
    xb_s, xz_s, xd_s, xp_r, xx_s, xx_r, xc_s, xc_r,
    w_s, w_r, b_s, b_r, z_s, z_r, gz_s, gz_r, g0_s, g1_s, g_r,
    a_s, a_r, c_s, c_r, rx_s, rx_r, l_s, l_r, f_s, f_r,
):
    o = lax.axis_index("outer")
    i = lax.axis_index("inner")
    h, y = o // 4, o % 4
    l, x, c = i // 8, (i // 2) % 4, i % 2
    pair, side = y // 2, y % 2
    h2, yb = 1 - h, 3 - y
    ya = pair * 2 + (1 - side)

    def at(hh, yy, ll, xx, cc):
        return (hh * 4 + yy, (ll * 4 + xx) * 2 + cc)

    dev_a = at(h, ya, l, x, c)
    dev_b = at(h, yb, l, x, c)
    dev_z = at(h2, y, l, x, c)
    dev_d = at(h2, yb, l, x, c)
    dev_c = at(h, y, l, x, 1 - c)
    dev_x = [at(h, y, l, (x + d) % 4, c) for d in (1, 2, 3)]
    dev_l = [at(h, y, (l + d) % 4, x, c) for d in (1, 2, 3)]

    barrier = pltpu.get_barrier_semaphore()
    everyone = [dev_a, dev_b, dev_z, dev_d, dev_c] + dev_x + dev_l
    for dev in everyone:
        pl.semaphore_signal(barrier, inc=1, device_id=dev, device_id_type=MESH)

    def remote(src, dst, s, r, dev):
        return pltpu.make_async_remote_copy(
            src_ref=src, dst_ref=dst, send_sem=s, recv_sem=r, device_id=dev, device_id_type=MESH
        )

    def root_l(t):
        return (1 - t // 4) * 3 * (t // 2) + t // 4 * (1 + t % 2)

    def root_c(t):
        return t % 2 + t // 6 * (1 - 2 * (t % 2))

    def columns(hh, pp):
        return pl.ds(pl.multiple_of((hh * 2 + pp) * DP, DP), DP)

    half = pl.ds(pl.multiple_of(c * DB, DB), DB)

    def half_columns(hh, pp):
        return pl.ds(pl.multiple_of((hh * 2 + pp) * DP + c * DB, DB), DB)

    def x_own(t):
        return pltpu.make_async_copy(
            x_hbm.at[root_l(t), :, root_c(t), :, columns(h, pair)], xs.at[t, OWN], sem_own
        )

    def x_push(t, cols, block, s, dev):
        return remote(
            x_hbm.at[root_l(t), x, root_c(t), :, cols], xs.at[t, block, x, :, half], s, xp_r.at[t], dev
        )

    def x_b(t):
        return x_push(t, half_columns(h, 1 - pair), BESIDE, xb_s, dev_b)

    def x_z(t):
        return x_push(t, half_columns(h2, pair), ACROSS, xz_s, dev_z)

    def x_d(t):
        return x_push(t, half_columns(h2, 1 - pair), DIAGONAL, xd_s, dev_d)

    def x_x(t, d):
        part = xs.at[t, 1:4, x, :, half]
        return remote(part, part, xx_s.at[d], xx_r.at[t], dev_x[d])

    def x_c(t):
        part = xs.at[t, 1:4, :, :, half]
        return remote(part, part, xc_s, xc_r.at[t], dev_c)

    w_rows = pl.ds(pl.multiple_of(side * DB, DB), DB)

    def f_cols(f):
        return pl.ds(pl.multiple_of(f * FC, FC), FC)

    def w_a(f):
        part = ws.at[f, w_rows]
        return remote(part, part, w_s, w_r.at[f], dev_a)

    def hid_b(k):
        return remote(send_b.at[k], recv_b.at[k], b_s, b_r.at[k], dev_b)

    def hid_z(k):
        return remote(send_z.at[k], recv_z.at[k], z_s, z_r.at[k], dev_z)

    def grad_z(k):
        return remote(hg.at[k, OWN], hg.at[k, ACROSS], gz_s, gz_r.at[k], dev_z)

    def grad_0(k):
        return remote(hg.at[k, OWN], hg.at[k, BESIDE], g0_s, g_r.at[k], dev_b)

    def grad_1(k):
        return remote(hg.at[k, ACROSS], hg.at[k, DIAGONAL], g1_s, g_r.at[k], dev_b)

    def term_a(f):
        return remote(send_a.at[f], recv_a.at[f], a_s, a_r.at[f], dev_a)

    def gw_out(f):
        return pltpu.make_async_copy(gout.at[f], gw_hbm.at[:, f_cols(f)], sem_gw)

    def red_c(n, s):
        return remote(send_c.at[n, :, HALVES[s]], recv_c.at[n, :, HALVES[s]], c_s, c_r.at[n, s], dev_c)

    def red_x(n, d, s):
        part = (n, d, slice(None), slice(None), HALVES[s])
        return remote(send_x.at[part], recv_x.at[part], rx_s.at[d], rx_r.at[n, s], dev_x[d])

    def red_l(n, s, away):
        part = send_l.at[n, :, :, HALVES[s]]
        return remote(
            part, recv_l.at[away - 1, :, :, HALVES[s]], l_s, l_r.at[away - 1, s], at(h, y, (l + 4 - away) % 4, x, c)
        )

    mine = h * 2 + pair

    def final(n, s):
        part = send_f.at[n, :, HALVES[s]]
        return remote(part, fin.at[mine, :, HALVES[s]], f_s, f_r, (dev_z, dev_d, dev_b)[n])

    def ig_out(n):
        return pltpu.make_async_copy(fin.at[n], ig_hbm.at[:, n * DP : (n + 1) * DP], sem_ig)

    codes_copy = pltpu.make_async_copy(codes_hbm, codes, sem_in.at[0])
    scales_copy = pltpu.make_async_copy(scales_hbm, scales, sem_in.at[1])
    act_copy = pltpu.make_async_copy(act_hbm, act, sem_in.at[2])
    scales_copy.start()
    codes_copy.start()
    for t in range(T):
        x_own(t).start()
    act_copy.start()
    pl.semaphore_wait(barrier, len(everyone))

    def x_start(t):
        x_d(t).start()
        x_z(t).start()
        x_b(t).start()

    def x_share(t):
        part = xs.at[t, 1:4, x, :, half]
        remote(part, part, xc_s, xp_r.at[t], dev_c).wait_recv()
        for d in range(3):
            x_x(t, d).start()

    def x_core(t):
        part = xs.at[t, 1:4, 0:3, :, half]
        remote(part, part, xc_s, xx_r.at[t], dev_c).wait_recv()
        x_c(t).start()

    x_start(0)
    x_start(1)
    scales_copy.wait()
    codes_copy.wait()
    scale = jnp.broadcast_to(scales[...].astype(F32).reshape(1, DB), (128, DB)).T
    for f in range(F):
        for j in range(FC // 128):
            value = codes[:, f * FC + j * 128 : f * FC + (j + 1) * 128].astype(F32) * scale
            ws[f, w_rows, j * 128 : (j + 1) * 128] = value.astype(BF16)
    w_a(0).start()
    w_a(1).start()
    x_start(2)
    w_a(2).start()
    for t in range(3, T):
        x_start(t)
    term[...] = jnp.zeros_like(term)
    x_share(0)
    act_copy.wait()
    pltpu.make_async_copy(xs.at[:, OWN], xs.at[:, OWN], sem_own).wait()
    x_share(1)
    x_core(0)
    x_share(2)
    x_core(1)

    def stage(step, offset, body):
        @pl.when((step >= offset) & (step < offset + K))
        def _():
            t, f = chunk(step - offset)
            body(t, f, t * F + f)

    def stage_t(step, offset, body):
        @pl.when((step >= offset) & (step < offset + K))
        def _():
            t, f = chunk(step - offset)

            @pl.when(f == F - 1)
            def _():
                body(t)

    def average(f):
        term_a(f).wait_recv()
        total = term[f, :, w_rows] + recv_a[f].astype(F32)
        gout[f] = total.T
        gw_out(f).start()

    def step_body(step, carry):
        def s4(t, f, k):
            hid_b(k).wait_recv()
            send_z[k] = (keep[k, 1] + recv_b[k, 0].astype(F32)).astype(BF16)
            hid_z(k).start()
            keep[k, 0] += recv_b[k, 1].astype(F32)

        stage(step, O_S4, s4)

        def s5(t, f, k):
            hid_z(k).wait_recv()
            hidden = keep[k, 0] + recv_z[k].astype(F32)
            given = act[root_l(t), :, root_c(t), :, f_cols(f)].reshape(TC, FC)
            hg[k, OWN] = (given.astype(F32) * gelu_slope(hidden)).astype(BF16)
            grad_z(k).start()
            grad_0(k).start()

        stage(step, O_S5, s5)

        def s6(t, f, k):
            grad_z(k).wait_recv()
            grad_1(k).start()

        stage(step, O_S6, s6)

        def s3(t, f, k):

            @pl.when(f == 0)
            def _():
                x_c(t).wait_recv()

            @pl.when(t == 0)
            def _():
                w_a(f).wait_recv()

            both = jnp.dot(xs[t].reshape(4 * TC, DP), ws[f], preferred_element_type=F32)
            send_b[k] = both[2 * TC :].astype(BF16).reshape(2, TC, FC)
            hid_b(k).start()
            keep[k] = both[: 2 * TC].reshape(2, TC, FC)

        stage(step, 0, s3)

        @pl.when(step == 0)
        def _():
            x_share(3)

        @pl.when(step < 2)
        def _():
            x_core(step + 2)

        @pl.when((step % 2 == 0) & (step >= 4) & (step <= 10))
        def _():
            x_share((step + 4) // 2)

        @pl.when((step % 2 == 0) & (step >= 6) & (step <= 12))
        def _():
            x_core((step + 2) // 2)

        def r1(t):
            n = t // 2

            @pl.when(c == root_c(t))
            def _():
                for s in range(2):
                    cols = HALVES[s]
                    red_c(n, s).wait_recv()
                    for d in (1, 2, 3, 0):
                        xx = (x + d) % 4
                        for block in range(4):
                            rows = pl.ds(pl.multiple_of(block * TC + xx * 16, 16), 16)
                            value = acc[t, rows, cols] + recv_c[n, rows, cols].astype(F32)
                            if d == 0:
                                keep_x[n, block, :, cols] = value
                            else:
                                send_x[n, d - 1, block, :, cols] = value.astype(BF16)
                        if d:
                            red_x(n, d - 1, s).start()

        stage_t(step, O_R1, r1)

        def s7(t, f, k):
            beside = hg.at[k, 2:4]
            remote(beside, beside, g0_s, g_r.at[k], dev_b).wait_recv()
            grads = hg[k].reshape(4 * TC, FC)

            def partial(cols):
                return lax.dot_general(
                    grads, ws[f, cols, :], (((1,), (1,)), ((), ())), preferred_element_type=F32
                )

            @pl.when(f == 0)
            def _():
                for j in range(DP // COLS):
                    cols = pl.ds(j * COLS, COLS)
                    acc[t, :, cols] = partial(cols)

            @pl.when((f > 0) & ((f < F - 1) | (c == root_c(t))))
            def _():
                for j in range(DP // COLS):
                    cols = pl.ds(j * COLS, COLS)
                    acc[t, :, cols] += partial(cols)

            @pl.when((f == F - 1) & (c != root_c(t)))
            def _():
                for s in range(2):
                    for j in range(DB // COLS):
                        cols = pl.ds(s * DB + j * COLS, COLS)
                        send_c[t // 2, :, cols] = (acc[t, :, cols] + partial(cols)).astype(BF16)
                    red_c(t // 2, s).start()

            for j in range(DP // COLS):
                cols = pl.ds(j * COLS, COLS)
                term[f, :, cols] += lax.dot_general(
                    grads, xs[t, :, :, :, cols].reshape(4 * TC, COLS),
                    (((0,), (0,)), ((), ())), preferred_element_type=F32,
                )

            @pl.when(t == T - 1)
            def _():
                other = pl.ds(pl.multiple_of((1 - side) * DB, DB), DB)
                send_a[f] = term[f, :, other].astype(BF16)
                term_a(f).start()

        stage(step, O_S7, s7)

        def r2(t):
            n = t // 2

            @pl.when(c == root_c(t))
            def _():
                for s in range(2):
                    cols = HALVES[s]
                    part = recv_x.at[n, :, :, :, cols]
                    remote(part, part, rx_s.at[0], rx_r.at[n, s], dev_c).wait_recv()
                    value = keep_x[n, :, :, cols]
                    for d in range(3):
                        value = value + recv_x[n, d, :, :, cols].astype(F32)
                    keep_x[n, :, :, cols] = value
                    send_l[n, :, :, cols] = value.astype(BF16)

                    for away in (1, 2, 3):

                        @pl.when((l - root_l(t) + 4) % 4 == away)
                        def _(s=s, away=away):
                            red_l(n, s, away).start()

        stage_t(step, O_R2, r2)

        return carry

    lax.fori_loop(0, STEPS, step_body, 0)

    for f in range(F - 1):
        average(f)

    last = l // 3 + (l + 1) // 2 % 2 * (2 + (l + c + 1) % 2)

    for s in range(2):
        cols = HALVES[s]

        value = keep_x[last, :, :, cols]
        for away in (1, 2, 3):
            red_l(0, s, away).wait_recv()
            value = value + recv_l[away - 1, :, :, cols].astype(F32)
        value = value.astype(BF16)
        fin[mine, :, cols] = value[OWN]
        for n in range(3):
            send_f[n, :, cols] = value[n + 1]
            final(n, s).start()

    average(F - 1)

    def left(buffer, s):
        remote(buffer, buffer, s, f_r, dev_c).wait_send()

    pushed = xs.at[:, BESIDE, x, :, half]
    for s in (xb_s, xz_s, xd_s):
        left(pushed, s)
    for d in range(3):
        left(xs.at[:, 1:4, x, :, half], xx_s.at[d])
        left(send_x.at[:, d], rx_s.at[d])
    left(xs.at[:, 1:4, :, :, half], xc_s)
    left(ws.at[:, w_rows], w_s)
    left(send_b, b_s)
    left(send_z, z_s)
    left(hg.at[:, OWN], gz_s)
    left(hg.at[:, OWN], g0_s)
    left(hg.at[:, ACROSS], g1_s)
    left(send_a, a_s)
    left(send_c, c_s)
    left(send_l.at[0:3], l_s)
    left(send_f, f_s)

    remote(fin.at[0:3], fin.at[0:3], f_s, f_r, dev_c).wait_recv()
    for n in range(4):
        ig_out(n).start()
    pltpu.make_async_copy(gout, gout, sem_gw).wait()
    pltpu.make_async_copy(fin, fin, sem_ig).wait()


def scratch():
    dma = pltpu.SemaphoreType.DMA
    return [
        pltpu.VMEM((T, 4, 4, 16, DP), BF16),
        pltpu.VMEM((F, DP, FC), BF16),
        pltpu.VMEM((DB, 768), BF16),
        pltpu.VMEM((DB,), BF16),
        pltpu.VMEM((4, 4, 2, 16, 768), BF16),
        pltpu.VMEM((K, 2, TC, FC), BF16),
        pltpu.VMEM((K, 2, TC, FC), BF16),
        pltpu.VMEM((K, 2, TC, FC), F32),
        pltpu.VMEM((K, TC, FC), BF16),
        pltpu.VMEM((K, TC, FC), BF16),
        pltpu.VMEM((K, 4, TC, FC), BF16),
        pltpu.VMEM((F, FC, DP), F32),
        pltpu.VMEM((T, 4 * TC, DP), F32),
        pltpu.VMEM((H, 4 * TC, DP), BF16),
        pltpu.VMEM((H, 4 * TC, DP), BF16),
        pltpu.VMEM((H, 3, 4, 16, DP), BF16),
        pltpu.VMEM((H, 3, 4, 16, DP), BF16),
        pltpu.VMEM((H, 4, 16, DP), F32),
        pltpu.VMEM((H, 4, 16, DP), BF16),
        pltpu.VMEM((3, 4, 16, DP), BF16),
        pltpu.VMEM((3, 16, DP), BF16),
        pltpu.VMEM((4, 16, DP), BF16),
        pltpu.VMEM((F, FC, DB), BF16),
        pltpu.VMEM((F, FC, DB), BF16),
        pltpu.VMEM((F, DB, FC), F32),
        dma, dma((3,)), dma, dma,
        dma, dma, dma, dma((T,)), dma((3,)), dma((T,)), dma, dma((T,)),
        dma, dma((F,)), dma, dma((K,)), dma, dma((K,)), dma, dma((K,)), dma, dma, dma((K,)),
        dma, dma((F,)), dma, dma((H, 2)), dma((3,)), dma((H, 2)), dma, dma((3, 2)), dma, dma,
    ]


def local(inputs, act_grad, in_codes, in_scales):
    input_grad, in_grad = pl.pallas_call(
        kernel,
        out_shape=(
            jax.ShapeDtypeStruct((16, 6144), BF16),
            jax.ShapeDtypeStruct((768, 768), F32),
        ),
        in_specs=[pl.BlockSpec(memory_space=pl.ANY)] * 4,
        out_specs=(
            pl.BlockSpec(memory_space=pl.ANY),
            pl.BlockSpec(memory_space=pl.ANY),
        ),
        scratch_shapes=scratch(),
        compiler_params=pltpu.CompilerParams(
            collective_id=0, has_side_effects=True, vmem_limit_bytes=60 * 1024 * 1024
        ),
        cost_estimate=pl.CostEstimate(
            flops=3 * 2 * 512 * 6144 * 768, bytes_accessed=12 * 1024 * 1024, transcendentals=512 * 768
        ),
        name="ffn_in_backward",
    )(
        inputs.reshape(4, 4, 2, 16, 6144),
        act_grad.reshape(4, 4, 2, 16, 768),
        in_codes,
        in_scales,
    )
    return input_grad, in_grad * 0.125


def solution(mesh):
    return jax.shard_map(
        local,
        mesh=mesh,
        in_specs=(P("outer", None), P("outer", "inner"), P("outer", "inner"), P("outer")),
        out_specs=(P(("outer", "inner"), None), P("outer", "inner")),
        check_vma=False,
    )
```

```python
import functools

import jax
import jax.numpy as jnp
from jax import lax
from jax.experimental import pallas as pl
from jax.experimental.pallas import tpu as pltpu
from jax.sharding import PartitionSpec as P

coef = 0.7978845608
cubic = 0.044715

MESH = pl.DeviceIdType.MESH
F32 = jnp.float32
BF16 = jnp.bfloat16

F = 3
H = 4
T = 2 * H
K = T * F
FC = 256
TC = 64
DB = 768
DP = 1536
COLS = 256
HALVES = (slice(0, DB), slice(DB, DP))
OWN, ACROSS, DIAGONAL, BESIDE = 0, 1, 2, 3

O_S4, O_S5, O_S6, O_S7, O_R1, O_R2 = 3, 6, 9, 12, 13, 24
STEPS = K + O_R2


def chunk(n):
    late = n // 12
    r = n % 12
    e = r // 6
    q = r % 6
    s = q // 2
    t = 4 + (1 - e) * (s // 2 * 2 + (1 - s % 2) * (q % 2)) + e * (1 + s)
    f = (1 - e) * (s % 2) * (1 + q % 2) + e * (1 + q % 2)
    return (1 - late) * (r % 4) + late * t, (1 - late) * (r // 4) + late * f


def gelu_slope(value):
    tangent = jnp.tanh(coef * (value + cubic * value * value * value))
    return 0.5 * (1.0 + tangent) + 0.5 * value * (1.0 - tangent * tangent) * coef * (
        1.0 + 3.0 * cubic * value * value
    )


def kernel(
    x_hbm, act_hbm, codes_hbm, scales_hbm, ig_hbm, gw_hbm,
    xs, ws, codes, scales, act, send_b, recv_b, keep, send_z, recv_z, hg, term,
    acc, send_c, recv_c, send_x, recv_x, keep_x, send_l, recv_l,
    send_f, fin, send_a, recv_a, gout,
    sem_own, sem_in, sem_gw, sem_ig,
    xb_s, xz_s, xd_s, xp_r, xx_s, xx_r, xc_s, xc_r,
    w_s, w_r, b_s, b_r, z_s, z_r, gz_s, gz_r, g0_s, g1_s, g_r,
    a_s, a_r, c_s, c_r, rx_s, rx_r, l_s, l_r, f_s, f_r,
):
    o = lax.axis_index("outer")
    i = lax.axis_index("inner")
    h, y = o // 4, o % 4
    l, x, c = i // 8, (i // 2) % 4, i % 2
    pair, side = y // 2, y % 2
    h2, yb = 1 - h, 3 - y
    ya = pair * 2 + (1 - side)

    def at(hh, yy, ll, xx, cc):
        return (hh * 4 + yy, (ll * 4 + xx) * 2 + cc)

    dev_a = at(h, ya, l, x, c)
    dev_b = at(h, yb, l, x, c)
    dev_z = at(h2, y, l, x, c)
    dev_d = at(h2, yb, l, x, c)
    dev_c = at(h, y, l, x, 1 - c)
    dev_x = [at(h, y, l, (x + d) % 4, c) for d in (1, 2, 3)]
    dev_l = [at(h, y, (l + d) % 4, x, c) for d in (1, 2, 3)]

    barrier = pltpu.get_barrier_semaphore()
    everyone = [dev_a, dev_b, dev_z, dev_d, dev_c] + dev_x + dev_l
    for dev in everyone:
        pl.semaphore_signal(barrier, inc=1, device_id=dev, device_id_type=MESH)

    def remote(src, dst, s, r, dev):
        return pltpu.make_async_remote_copy(
            src_ref=src, dst_ref=dst, send_sem=s, recv_sem=r, device_id=dev, device_id_type=MESH
        )

    def root_l(t):
        return (1 - t // 4) * 3 * (t // 2) + t // 4 * (1 + t % 2)

    def root_c(t):
        return t % 2 + t // 6 * (1 - 2 * (t % 2))

    def columns(hh, pp):
        return pl.ds(pl.multiple_of((hh * 2 + pp) * DP, DP), DP)

    half = pl.ds(pl.multiple_of(c * DB, DB), DB)

    def half_columns(hh, pp):
        return pl.ds(pl.multiple_of((hh * 2 + pp) * DP + c * DB, DB), DB)

    def x_own(t):
        return pltpu.make_async_copy(
            x_hbm.at[root_l(t), :, root_c(t), :, columns(h, pair)], xs.at[t, OWN], sem_own
        )

    def x_push(t, cols, block, s, dev):
        return remote(
            x_hbm.at[root_l(t), x, root_c(t), :, cols], xs.at[t, block, x, :, half], s, xp_r.at[t], dev
        )

    def x_b(t):
        return x_push(t, half_columns(h, 1 - pair), BESIDE, xb_s, dev_b)

    def x_z(t):
        return x_push(t, half_columns(h2, pair), ACROSS, xz_s, dev_z)

    def x_d(t):
        return x_push(t, half_columns(h2, 1 - pair), DIAGONAL, xd_s, dev_d)

    def x_x(t, d):
        part = xs.at[t, 1:4, x, :, half]
        return remote(part, part, xx_s.at[d], xx_r.at[t], dev_x[d])

    def x_c(t):
        part = xs.at[t, 1:4, :, :, half]
        return remote(part, part, xc_s, xc_r.at[t], dev_c)

    w_rows = pl.ds(pl.multiple_of(side * DB, DB), DB)

    def f_cols(f):
        return pl.ds(pl.multiple_of(f * FC, FC), FC)

    def w_a(f):
        part = ws.at[f, w_rows]
        return remote(part, part, w_s, w_r.at[f], dev_a)

    def hid_b(k):
        return remote(send_b.at[k], recv_b.at[k], b_s, b_r.at[k], dev_b)

    def hid_z(k):
        return remote(send_z.at[k], recv_z.at[k], z_s, z_r.at[k], dev_z)

    def grad_z(k):
        return remote(hg.at[k, OWN], hg.at[k, ACROSS], gz_s, gz_r.at[k], dev_z)

    def grad_0(k):
        return remote(hg.at[k, OWN], hg.at[k, BESIDE], g0_s, g_r.at[k], dev_b)

    def grad_1(k):
        return remote(hg.at[k, ACROSS], hg.at[k, DIAGONAL], g1_s, g_r.at[k], dev_b)

    def term_a(f):
        return remote(send_a.at[f], recv_a.at[f], a_s, a_r.at[f], dev_a)

    def gw_out(f):
        return pltpu.make_async_copy(gout.at[f], gw_hbm.at[:, f_cols(f)], sem_gw)

    def red_c(n, s):
        return remote(send_c.at[n, :, HALVES[s]], recv_c.at[n, :, HALVES[s]], c_s, c_r.at[n, s], dev_c)

    def red_x(n, d, s):
        part = (n, d, slice(None), slice(None), HALVES[s])
        return remote(send_x.at[part], recv_x.at[part], rx_s.at[d], rx_r.at[n, s], dev_x[d])

    def red_l(n, s, away):
        part = send_l.at[n, :, :, HALVES[s]]
        return remote(
            part, recv_l.at[away - 1, :, :, HALVES[s]], l_s, l_r.at[away - 1, s], at(h, y, (l + 4 - away) % 4, x, c)
        )

    mine = h * 2 + pair

    def final(n, s):
        part = send_f.at[n, :, HALVES[s]]
        return remote(part, fin.at[mine, :, HALVES[s]], f_s, f_r, (dev_z, dev_d, dev_b)[n])

    def ig_out(n):
        return pltpu.make_async_copy(fin.at[n], ig_hbm.at[:, n * DP : (n + 1) * DP], sem_ig)

    codes_copy = pltpu.make_async_copy(codes_hbm, codes, sem_in.at[0])
    scales_copy = pltpu.make_async_copy(scales_hbm, scales, sem_in.at[1])
    act_copy = pltpu.make_async_copy(act_hbm, act, sem_in.at[2])
    scales_copy.start()
    codes_copy.start()
    for t in range(T):
        x_own(t).start()
    act_copy.start()
    pl.semaphore_wait(barrier, len(everyone))

    def x_start(t):
        x_d(t).start()
        x_z(t).start()
        x_b(t).start()

    def x_share(t):
        part = xs.at[t, 1:4, x, :, half]
        remote(part, part, xc_s, xp_r.at[t], dev_c).wait_recv()
        for d in (1, 0, 2):
            x_x(t, d).start()

    def x_core(t):
        part = xs.at[t, 1:4, 0:3, :, half]
        remote(part, part, xc_s, xx_r.at[t], dev_c).wait_recv()
        x_c(t).start()

    x_start(0)
    x_start(1)
    scales_copy.wait()
    codes_copy.wait()
    scale = jnp.broadcast_to(scales[...].astype(F32).reshape(1, DB), (128, DB)).T
    for f in range(F):
        for j in range(FC // 128):
            value = codes[:, f * FC + j * 128 : f * FC + (j + 1) * 128].astype(F32) * scale
            ws[f, w_rows, j * 128 : (j + 1) * 128] = value.astype(BF16)
    w_a(0).start()
    w_a(1).start()
    x_start(2)
    w_a(2).start()
    for t in range(3, T):
        x_start(t)
    term[...] = jnp.zeros_like(term)
    x_share(0)
    act_copy.wait()
    pltpu.make_async_copy(xs.at[:, OWN], xs.at[:, OWN], sem_own).wait()
    x_share(1)
    x_core(0)
    x_share(2)
    x_core(1)

    def stage(step, offset, body):
        @pl.when((step >= offset) & (step < offset + K))
        def _():
            t, f = chunk(step - offset)
            body(t, f, t * F + f)

    def stage_t(step, offset, body):
        @pl.when((step >= offset) & (step < offset + K))
        def _():
            t, f = chunk(step - offset)

            @pl.when(f == F - 1)
            def _():
                body(t)

    def average(f):
        term_a(f).wait_recv()
        total = term[f, :, w_rows] + recv_a[f].astype(F32)
        gout[f] = total.T
        gw_out(f).start()

    def step_body(step, carry):
        def s4(t, f, k):
            hid_b(k).wait_recv()
            send_z[k] = (keep[k, 1] + recv_b[k, 0].astype(F32)).astype(BF16)
            hid_z(k).start()
            keep[k, 0] += recv_b[k, 1].astype(F32)

        stage(step, O_S4, s4)

        def s5(t, f, k):
            hid_z(k).wait_recv()
            hidden = keep[k, 0] + recv_z[k].astype(F32)
            given = act[root_l(t), :, root_c(t), :, f_cols(f)].reshape(TC, FC)
            hg[k, OWN] = (given.astype(F32) * gelu_slope(hidden)).astype(BF16)
            grad_z(k).start()
            grad_0(k).start()

        stage(step, O_S5, s5)

        def s6(t, f, k):
            grad_z(k).wait_recv()
            grad_1(k).start()

        stage(step, O_S6, s6)

        def s3(t, f, k):

            @pl.when(f == 0)
            def _():
                x_c(t).wait_recv()

            @pl.when(t == 0)
            def _():
                w_a(f).wait_recv()

            both = jnp.dot(xs[t].reshape(4 * TC, DP), ws[f], preferred_element_type=F32)
            send_b[k] = both[2 * TC :].astype(BF16).reshape(2, TC, FC)
            hid_b(k).start()
            keep[k] = both[: 2 * TC].reshape(2, TC, FC)

        stage(step, 0, s3)

        @pl.when(step == 0)
        def _():
            x_share(3)

        @pl.when(step < 2)
        def _():
            x_core(step + 2)

        @pl.when((step % 2 == 0) & (step >= 4) & (step <= 10))
        def _():
            x_share((step + 4) // 2)

        @pl.when((step % 2 == 0) & (step >= 6) & (step <= 12))
        def _():
            x_core((step + 2) // 2)

        def r1(t):
            n = t // 2

            @pl.when(c == root_c(t))
            def _():
                for s in range(2):
                    cols = HALVES[s]
                    red_c(n, s).wait_recv()
                    for d in (2, 1, 3, 0):
                        xx = (x + d) % 4
                        for block in range(4):
                            rows = pl.ds(pl.multiple_of(block * TC + xx * 16, 16), 16)
                            value = acc[n, rows, cols] + recv_c[n, rows, cols].astype(F32)
                            if d == 0:
                                keep_x[n, block, :, cols] = value
                            else:
                                send_x[n, d - 1, block, :, cols] = value.astype(BF16)
                        if d:
                            red_x(n, d - 1, s).start()

        stage_t(step, O_R1, r1)

        def s7(t, f, k):
            beside = hg.at[k, 2:4]
            remote(beside, beside, g0_s, g_r.at[k], dev_b).wait_recv()
            grads = hg[k].reshape(4 * TC, FC)

            def partial(cols):
                return sum(
                    lax.dot_general(
                        hg[t * F + n].reshape(4 * TC, FC), ws[n, cols, :],
                        (((1,), (1,)), ((), ())), preferred_element_type=F32,
                    )
                    for n in range(F)
                )

            @pl.when((f == F - 1) & (c == root_c(t)))
            def _():
                for j in range(DP // COLS):
                    cols = pl.ds(j * COLS, COLS)
                    acc[t // 2, :, cols] = partial(cols)

            @pl.when((f == F - 1) & (c != root_c(t)))
            def _():
                for s in range(2):
                    for j in range(DB // COLS):
                        cols = pl.ds(s * DB + j * COLS, COLS)
                        send_c[t // 2, :, cols] = partial(cols).astype(BF16)
                    red_c(t // 2, s).start()

            for j in range(DP // COLS):
                cols = pl.ds(j * COLS, COLS)
                term[f, :, cols] += lax.dot_general(
                    grads, xs[t, :, :, :, cols].reshape(4 * TC, COLS),
                    (((0,), (0,)), ((), ())), preferred_element_type=F32,
                )

            @pl.when(t == T - 1)
            def _():
                other = pl.ds(pl.multiple_of((1 - side) * DB, DB), DB)
                send_a[f] = term[f, :, other].astype(BF16)
                term_a(f).start()

        stage(step, O_S7, s7)

        def r2(t):
            n = t // 2

            @pl.when(c == root_c(t))
            def _():
                for s in range(2):
                    cols = HALVES[s]
                    part = recv_x.at[n, :, :, :, cols]
                    remote(part, part, rx_s.at[0], rx_r.at[n, s], dev_c).wait_recv()
                    value = keep_x[n, :, :, cols]
                    for d in range(3):
                        value = value + recv_x[n, d, :, :, cols].astype(F32)
                    keep_x[n, :, :, cols] = value
                    send_l[n, :, :, cols] = value.astype(BF16)

                    for away in (1, 2, 3):

                        @pl.when((l - root_l(t) + 4) % 4 == away)
                        def _(s=s, away=away):
                            red_l(n, s, away).start()

        stage_t(step, O_R2, r2)

        return carry

    lax.fori_loop(0, STEPS, step_body, 0)

    for f in range(F - 1):
        average(f)

    last = l // 3 + (l + 1) // 2 % 2 * (2 + (l + c + 1) % 2)

    for s in range(2):
        cols = HALVES[s]

        value = keep_x[last, :, :, cols]
        for away in (1, 2, 3):
            red_l(0, s, away).wait_recv()
            value = value + recv_l[away - 1, :, :, cols].astype(F32)
        value = value.astype(BF16)
        fin[mine, :, cols] = value[OWN]
        for n in (1, 0, 2):
            send_f[n, :, cols] = value[n + 1]
            final(n, s).start()

    average(F - 1)

    def left(buffer, s):
        remote(buffer, buffer, s, f_r, dev_c).wait_send()

    pushed = xs.at[:, BESIDE, x, :, half]
    for s in (xb_s, xz_s, xd_s):
        left(pushed, s)
    for d in range(3):
        left(xs.at[:, 1:4, x, :, half], xx_s.at[d])
        left(send_x.at[:, d], rx_s.at[d])
    left(xs.at[:, 1:4, :, :, half], xc_s)
    left(ws.at[:, w_rows], w_s)
    left(send_b, b_s)
    left(send_z, z_s)
    left(hg.at[:, OWN], gz_s)
    left(hg.at[:, OWN], g0_s)
    left(hg.at[:, ACROSS], g1_s)
    left(send_a, a_s)
    left(send_c, c_s)
    left(send_l.at[0:3], l_s)
    left(send_f, f_s)

    remote(fin.at[0:3], fin.at[0:3], f_s, f_r, dev_c).wait_recv()
    for n in range(4):
        ig_out(n).start()
    pltpu.make_async_copy(gout, gout, sem_gw).wait()
    pltpu.make_async_copy(fin, fin, sem_ig).wait()


def scratch():
    dma = pltpu.SemaphoreType.DMA
    return [
        pltpu.VMEM((T, 4, 4, 16, DP), BF16),
        pltpu.VMEM((F, DP, FC), BF16),
        pltpu.VMEM((DB, 768), BF16),
        pltpu.VMEM((DB,), BF16),
        pltpu.VMEM((4, 4, 2, 16, 768), BF16),
        pltpu.VMEM((K, 2, TC, FC), BF16),
        pltpu.VMEM((K, 2, TC, FC), BF16),
        pltpu.VMEM((K, 2, TC, FC), F32),
        pltpu.VMEM((K, TC, FC), BF16),
        pltpu.VMEM((K, TC, FC), BF16),
        pltpu.VMEM((K, 4, TC, FC), BF16),
        pltpu.VMEM((F, FC, DP), F32),
        pltpu.VMEM((H, 4 * TC, DP), F32),
        pltpu.VMEM((H, 4 * TC, DP), BF16),
        pltpu.VMEM((H, 4 * TC, DP), BF16),
        pltpu.VMEM((H, 3, 4, 16, DP), BF16),
        pltpu.VMEM((H, 3, 4, 16, DP), BF16),
        pltpu.VMEM((H, 4, 16, DP), F32),
        pltpu.VMEM((H, 4, 16, DP), BF16),
        pltpu.VMEM((3, 4, 16, DP), BF16),
        pltpu.VMEM((3, 16, DP), BF16),
        pltpu.VMEM((4, 16, DP), BF16),
        pltpu.VMEM((F, FC, DB), BF16),
        pltpu.VMEM((F, FC, DB), BF16),
        pltpu.VMEM((F, DB, FC), F32),
        dma, dma((3,)), dma, dma,
        dma, dma, dma, dma((T,)), dma((3,)), dma((T,)), dma, dma((T,)),
        dma, dma((F,)), dma, dma((K,)), dma, dma((K,)), dma, dma((K,)), dma, dma, dma((K,)),
        dma, dma((F,)), dma, dma((H, 2)), dma((3,)), dma((H, 2)), dma, dma((3, 2)), dma, dma,
    ]


def local(inputs, act_grad, in_codes, in_scales):
    input_grad, in_grad = pl.pallas_call(
        kernel,
        out_shape=(
            jax.ShapeDtypeStruct((16, 6144), BF16),
            jax.ShapeDtypeStruct((768, 768), F32),
        ),
        in_specs=[pl.BlockSpec(memory_space=pl.ANY)] * 4,
        out_specs=(
            pl.BlockSpec(memory_space=pl.ANY),
            pl.BlockSpec(memory_space=pl.ANY),
        ),
        scratch_shapes=scratch(),
        compiler_params=pltpu.CompilerParams(
            collective_id=0, has_side_effects=True, vmem_limit_bytes=60 * 1024 * 1024
        ),
        cost_estimate=pl.CostEstimate(
            flops=3 * 2 * 512 * 6144 * 768, bytes_accessed=12 * 1024 * 1024, transcendentals=512 * 768
        ),
        name="ffn_in_backward",
    )(
        inputs.reshape(4, 4, 2, 16, 6144),
        act_grad.reshape(4, 4, 2, 16, 768),
        in_codes,
        in_scales,
    )
    return input_grad, in_grad * 0.125


def solution(mesh):
    return jax.shard_map(
        local,
        mesh=mesh,
        in_specs=(P("outer", None), P("outer", "inner"), P("outer", "inner"), P("outer")),
        out_specs=(P(("outer", "inner"), None), P("outer", "inner")),
        check_vma=False,
    )
```
